128 devices in a mesh: dp: 64 (over x, y, z), tensor: 2 (over core).
Axes of the slice: x: 4, y: 4, z: 4, core: 2. Of those that a mesh axis runs over, the one named last changes fastest.
Arguments:
- momentum: float32 [64, 768, 2560], P(None, ('dp', 'tensor')), may hold values from -6 to 6
- gradient: bfloat16 [64, 768, 2560], P(None, ('dp', 'tensor'))
- assignment: int32 [64], replicated, may hold values from -1 to 63, as said below
Outputs:
- momentum_new: float32 [64, 768, 2560], P(None, ('dp', 'tensor'))
- update: bfloat16 [64, 768, 2560], P(None, ('dp', 'tensor'))
The draws below stay inside these ranges and needn't reach their ends.
Inputs may be any that keep to these rules, and one draw needn't show every extreme that they name: `assignment`: entry m is the owner of matrix m along dp, or -1 where matrix m takes no update at this step. No owner holds more than 3 matrices, and some owner holds exactly 3.
All inputs are finite; a program needn't handle non-finite values.
Results may differ from the reference program's by a relative error of at most 0.0017.
The reference program's roundings to bfloat16 on the way count: a program that leaves them out, or rounds other values in their place, can miss the bound.
Values may be sent and summed in bfloat16 or wider, within the bound.
A program may use at most 128 MiB of HBM per device.

```python
import math
import jax
import jax.numpy as jnp
from jax import lax

D = 2560
F = 768
MOST = 3
ITERS = 2
MATRICES = 64
N_DP = 64


def draw_gradient(key, part):
    key = jax.random.fold_in(key, 5)
    key_base, key_cols = jax.random.split(key, 2)
    row_scale = jnp.exp(jnp.arange(F, dtype=jnp.float32) * (math.log(10.0) / F))
    col_scale = jnp.exp(jax.random.uniform(key_cols, (MATRICES, 1, D), jnp.float32, 0.0, math.log(10.0)))
    base = jax.random.normal(key_base, (MATRICES, F, D), jnp.float32)
    return (base * row_scale[None, :, None] * col_scale).astype(jnp.bfloat16)


def draw_assignment(key, part):
    key = jax.random.fold_in(key, 11)
    key_busy, key_slots, key_mats = jax.random.split(key, 3)
    busiest = jax.random.randint(key_busy, (), 0, N_DP)
    slot_ids = jax.random.permutation(key_slots, N_DP * MOST).astype(jnp.int32)
    priority = jnp.where(slot_ids // MOST == busiest, 0, 1).astype(jnp.int32)
    sorted_slots = slot_ids[jnp.argsort(priority, stable=True)]
    live_count = MATRICES - MATRICES // 4
    positions = jnp.arange(MATRICES, dtype=jnp.int32)
    owner_sorted = jnp.where(positions < live_count, sorted_slots[:MATRICES] // MOST, -1).astype(jnp.int32)
    matrix_order = jax.random.permutation(key_mats, MATRICES).astype(jnp.int32)
    return jnp.zeros((MATRICES,), jnp.int32).at[matrix_order].set(owner_sorted)


def block_levels(own_key, extent, shards, least, largest):
    loudness, own = 1.0, jax.random.fold_in(own_key, 6)
    for axis_at, blocks in shards:
        heights = jnp.exp(jax.random.uniform(jax.random.fold_in(own, axis_at), (blocks,), jnp.float32, least / len(shards), largest / len(shards)))
        loudness = loudness * jnp.repeat(heights, extent[axis_at] // blocks).reshape([-1 if axis == axis_at else 1 for axis in range(len(extent))])
    return loudness


def noise(rng, dims, width, most, shards=(), held_as=jnp.bfloat16):
    factor_of = block_levels(rng, dims, shards, -0.22, 0.18) if shards else 1.0
    values = jax.random.normal(rng, dims, jnp.float32) * width * factor_of
    return jnp.minimum(jnp.maximum(values, -most), most).astype(held_as)


def setup_inputs(seed: int = 0) -> dict:
    key_list = jax.random.split(jax.random.key(seed), 4)
    return {
        "momentum": noise(key_list[0], (MATRICES, F, D), 1.0, 6.0, ((1, 128),), jnp.float32),
        "gradient": draw_gradient(jax.random.fold_in(key_list[3], 71), 0),
        "assignment": draw_assignment(jax.random.fold_in(key_list[3], 71), 0),
    }


momentum_rate = 0.95
epsilon_norm = 1e-07
linear_term = 3.4445
cubic_term = -4.775
quintic_term = 2.0315

def orthogonalize_one(direction):
    values = direction.astype(jnp.float32)
    total = jnp.sum(values * values)
    matrix_now = (values / (jnp.sqrt(total) + epsilon_norm)).astype(jnp.bfloat16)
    for repeat in range(ITERS):
        gram_rows = jnp.dot(matrix_now, matrix_now.T, preferred_element_type=jnp.float32)
        gram_low = gram_rows.astype(jnp.bfloat16)
        mixer_rows = (cubic_term * gram_rows + quintic_term * jnp.dot(gram_low, gram_low, preferred_element_type=jnp.float32)).astype(jnp.bfloat16)
        matrix_now = (linear_term * matrix_now.astype(jnp.float32) + jnp.dot(mixer_rows, matrix_now, preferred_element_type=jnp.float32)).astype(jnp.bfloat16)
    return matrix_now

def reference(momentum, gradient, assignment):
    momentum_new = momentum_rate * momentum + gradient.astype(jnp.float32)
    direction = (gradient.astype(jnp.float32) + momentum_rate * momentum_new).astype(jnp.bfloat16)
    result = lax.map(orthogonalize_one, direction)
    active = assignment >= 0
    update_scale = math.sqrt(D)
    update = jnp.where(active[:, None, None], update_scale * result.astype(jnp.float32), jnp.float32(0.0)).astype(jnp.bfloat16)
    return (momentum_new, update)
```

```python
import math

import jax
import jax.numpy as jnp
from jax import lax
from jax.sharding import PartitionSpec as P

ITERS = 2


momentum_rate = 0.95
epsilon_norm = 1e-07
linear_term = 3.4445
cubic_term = -4.775
quintic_term = 2.0315


def newton_schulz(matrix_part):
    for repeat in range(ITERS):
        whole_rows = lax.all_gather(matrix_part, "tensor", axis=1, tiled=True)
        gram_rows = jnp.einsum(
            "kid,kjd->kij", matrix_part, whole_rows, preferred_element_type=jnp.float32
        )
        gram_low = gram_rows.astype(jnp.bfloat16)
        gram_whole = lax.all_gather(gram_low, "tensor", axis=1, tiled=True)
        square = jnp.einsum(
            "kij,kjl->kil", gram_low, gram_whole, preferred_element_type=jnp.float32
        )
        mixer_rows = (cubic_term * gram_rows + quintic_term * square).astype(jnp.bfloat16)
        product = jnp.einsum(
            "kij,kjd->kid", mixer_rows, whole_rows, preferred_element_type=jnp.float32
        )
        matrix_part = (linear_term * matrix_part.astype(jnp.float32) + product).astype(jnp.bfloat16)
    return matrix_part


def orthogonalize(arrived):
    item_count, source_count, row_count, col_count = arrived.shape
    matrix_part = arrived.reshape(item_count, source_count * row_count, col_count)
    squares = jnp.sum(jnp.square(matrix_part.astype(jnp.float32)), axis=(1, 2))
    totals = lax.psum(squares, "tensor")
    matrix_part = (
        matrix_part.astype(jnp.float32) / (jnp.sqrt(totals) + epsilon_norm)[:, None, None]
    ).astype(jnp.bfloat16)
    result = newton_schulz(matrix_part)
    return lax.all_to_all(
        result.reshape(item_count, source_count, row_count, col_count),
        "dp",
        split_axis=1,
        concat_axis=1,
        tiled=True,
    )


def on_device(momentum, gradient, assignment):
    wide = gradient.astype(jnp.float32)
    momentum_new = momentum_rate * momentum + wide
    direction = (wide + momentum_rate * momentum_new).astype(jnp.bfloat16)
    arrived = lax.all_to_all(direction, "dp", split_axis=0, concat_axis=0, tiled=True)
    returned = orthogonalize(arrived[None])[0]
    update_scale = math.sqrt(momentum.shape[2])
    update = jnp.where(
        (assignment >= 0)[:, None, None], update_scale * returned.astype(jnp.float32), jnp.float32(0.0)
    ).astype(jnp.bfloat16)
    return (momentum_new, update)


def solution(mesh):
    placed = (P(None, ("dp", "tensor"), None), P(None, ("dp", "tensor"), None), P())
    return jax.shard_map(
        on_device,
        mesh=mesh,
        in_specs=placed,
        out_specs=(P(None, ("dp", "tensor"), None), P(None, ("dp", "tensor"), None)),
        check_vma=False,
    )
```

```python
import functools
import math

import jax
import jax.numpy as jnp
from jax import lax
from jax.experimental import pallas as pl
from jax.experimental.pallas import tpu as pltpu
from jax.sharding import PartitionSpec as P

ITERS = 2
MESH = pl.DeviceIdType.MESH

momentum_rate = 0.95
epsilon_norm = 1e-07
linear_term = 3.4445
cubic_term = -4.775
quintic_term = 2.0315

SIDE = 4
CHIPS = SIDE**3
LOCAL = 6
WIDTH = 2560
LANES = 128
TILES = WIDTH // LANES
ROWS = LOCAL * CHIPS * 2
HALF = LOCAL * CHIPS
LINES = LOCAL * TILES
BLOCK = (8, LINES // 8 * LANES)
PITCH = LINES + 1
GROUP = 16
GROUPS = CHIPS // GROUP
HALVES = 2
SLOTS = CHIPS // HALVES
STEP = 512
TILE = 256
STRIPS = ROWS // TILE
STRIDE = 27


def position():
    return lax.axis_index("dp"), lax.axis_index("tensor")


def moved(index, sign):
    place, _ = position()
    offset = index * STRIDE % CHIPS
    spot = 0
    for scale in (SIDE * SIDE, SIDE, 1):
        here = place // scale % SIDE
        away = offset // scale % SIDE
        spot = spot + (here + sign * away + SIDE) % SIDE * scale
    return spot


def line_of(row, tile):
    return tile * LOCAL + row


def write_lines(scratch, row, tile, values):
    scratch[pl.ds(line_of(row, tile), 8, stride=PITCH), :] = values


def read_lines(scratch, row, tile):
    return scratch[pl.ds(line_of(row, tile), 8, stride=PITCH), :]


def pack_eight(scratch, blocks, first):
    for item in range(8):
        for part in range(LINES // 8):
            values = scratch[pl.ds(item * PITCH + 8 * part, 8), :]
            blocks[first + item, :, part * LANES : (part + 1) * LANES] = values.astype(jnp.bfloat16)


def unpack_eight(scratch, blocks, first):
    for item in range(8):
        values = blocks[first + item].astype(jnp.float32)
        for part in range(LINES // 8):
            scratch[pl.ds(item * PITCH + 8 * part, 8), :] = values[:, part * LANES : (part + 1) * LANES]


def product(a, b, dims):
    return lax.dot_general(a, b, (dims, ((), ())), preferred_element_type=jnp.float32)


def strip(index):
    return slice(index * TILE, (index + 1) * TILE)


def gram_of(x_ref, gram, low):
    for i in range(STRIPS):
        for j in range(i + 1):
            value = product(x_ref[strip(i), :], x_ref[strip(j), :], ((1,), (1,)))
            gram[strip(i), strip(j)] = value
            rounded = value.astype(jnp.bfloat16)
            low[strip(i), strip(j)] = rounded
            if i != j:
                low[strip(j), strip(i)] = value.T.astype(jnp.bfloat16)


def mixer_of(gram, low, mixer):
    for j in range(STRIPS):
        for i in range(j, STRIPS):
            square = product(low[strip(i), :], low[:, strip(j)], ((1,), (0,)))
            value = cubic_term * gram[strip(i), strip(j)] + quintic_term * square
            mixer[strip(i), strip(j)] = value.astype(jnp.bfloat16)
            if i != j:
                mixer[strip(j), strip(i)] = value.T.astype(jnp.bfloat16)


def kernel(
    momentum, gradient, assignment, momentum_new, update,
    mom_in, grad_in, sent, arrived, returned, x_now, x_next, gram, low, mixer, lines, squares, squares_in,
    load_sems, out_sem, in_sems, back_out_sem, back_sems, pair_out_sem, pair_sems, square_sems,
):
    place, core = position()
    pair = (place, 1 - core)

    def load(group):
        rows = pl.ds(pl.multiple_of(group * GROUP, GROUP), GROUP)
        return (
            pltpu.make_async_copy(momentum.at[:, rows, :], mom_in.at[group], load_sems.at[0, group]),
            pltpu.make_async_copy(gradient.at[:, rows, :], grad_in.at[group], load_sems.at[1, group]),
        )

    for group in range(GROUPS):
        for copy in load(group):
            copy.start()

    barrier = pltpu.get_barrier_semaphore()
    pl.semaphore_signal(barrier, inc=1, device_id=pair, device_id_type=MESH)

    def greet(index, carry):
        pl.semaphore_signal(barrier, inc=1, device_id=(moved(index, 1), core), device_id_type=MESH)
        return carry

    lax.fori_loop(1, CHIPS, greet, 0)

    def prepare(group, carry):
        for copy in load(group):
            copy.wait()
        rows = pl.ds(pl.multiple_of(group * GROUP, GROUP), GROUP)
        for row in range(LOCAL):
            for tile in range(TILES):
                columns = slice(tile * LANES, (tile + 1) * LANES)
                wide = grad_in[group, row, :, columns].astype(jnp.float32)
                fresh = momentum_rate * mom_in[group, row, :, columns] + wide
                momentum_new[row, rows, columns] = fresh
                direction = wide + momentum_rate * fresh
                for eight in range(2):
                    write_lines(lines.at[eight], row, tile, direction[eight * 8 : eight * 8 + 8])
        for eight in range(2):
            pack_eight(lines.at[eight], sent, group * GROUP + eight * 8)
        return carry

    lax.fori_loop(0, GROUPS, prepare, 0)

    pl.semaphore_wait(barrier, CHIPS)

    pltpu.make_async_copy(sent.at[place], arrived.at[0], in_sems.at[0]).start()

    def send(index, carry):
        target = moved(index, 1)
        pltpu.make_async_remote_copy(
            src_ref=sent.at[target], dst_ref=arrived.at[index], send_sem=out_sem, recv_sem=in_sems.at[index // GROUP],
            device_id=(target, core), device_id_type=MESH,
        ).start()
        return carry

    lax.fori_loop(1, CHIPS, send, 0)

    def rows_of(group, row):
        start = group // (GROUPS // HALVES) * (LOCAL * SLOTS) + row * SLOTS + group % (GROUPS // HALVES) * GROUP
        return pl.multiple_of(start, GROUP)

    def relay(group, row):
        start = rows_of(group, row)
        return pltpu.make_async_remote_copy(
            src_ref=x_now.at[pl.ds(start, GROUP), :], dst_ref=x_now.at[pl.ds(HALF + start, GROUP), :],
            send_sem=pair_out_sem, recv_sem=pair_sems.at[0], device_id=pair, device_id_type=MESH,
        )

    squares[...] = jnp.zeros_like(squares)

    def accept(group, carry):
        span = arrived.at[pl.ds(group * GROUP, GROUP)]
        pltpu.make_async_copy(span, span, in_sems.at[group]).wait()
        for eight in range(2):
            unpack_eight(lines.at[eight], arrived, group * GROUP + eight * 8)
        for row in range(LOCAL):
            start = rows_of(group, row)
            total = jnp.zeros((8, LANES), jnp.float32)
            for tile in range(TILES):
                values = [read_lines(lines.at[eight], row, tile) for eight in range(2)]
                for value in values:
                    total += value * value
                x_now[pl.ds(start, GROUP), tile * LANES : (tile + 1) * LANES] = jnp.concatenate(
                    values, axis=0
                ).astype(jnp.bfloat16)
            squares[...] += total
            relay(group, row).start()
        return carry

    lax.fori_loop(0, GROUPS, accept, 0)

    swap = pltpu.make_async_remote_copy(
        src_ref=squares, dst_ref=squares_in, send_sem=square_sems.at[0], recv_sem=square_sems.at[1],
        device_id=pair, device_id_type=MESH,
    )
    swap.start()
    swap.wait()
    own, other = x_now.at[pl.ds(0, HALF), :], x_now.at[pl.ds(HALF, HALF), :]
    pltpu.make_async_copy(own, own, pair_out_sem).wait()
    pltpu.make_async_copy(other, other, pair_sems.at[0]).wait()

    norm = jnp.sqrt(jnp.sum(squares[...] + squares_in[...])) + epsilon_norm

    def normalize(index, carry):
        rows = pl.ds(pl.multiple_of(index * 32, 32), 32)
        x_now[rows, :] = (x_now[rows, :].astype(jnp.float32) / norm).astype(jnp.bfloat16)
        return carry

    lax.fori_loop(0, ROWS // 32, normalize, 0)

    gram_of(x_now, gram, low)
    mixer_of(gram, low, mixer)

    def mix(index, carry):
        columns = pl.ds(pl.multiple_of(index * STEP, STEP), STEP)
        for i in range(STRIPS):
            value = product(mixer[strip(i), :], x_now[:, columns], ((1,), (0,)))
            x_next[strip(i), columns] = (
                linear_term * x_now[strip(i), columns].astype(jnp.float32) + value
            ).astype(jnp.bfloat16)
        return carry

    lax.fori_loop(0, WIDTH // STEP, mix, 0)

    gram_of(x_next, gram, low)
    mixer_of(gram, low, mixer)

    active = assignment[place] >= 0
    part = LOCAL * SLOTS

    def finish(half, carry):
        rows = pl.ds(pl.multiple_of(half * part, part), part)

        def columns_step(index, inner):
            columns = pl.ds(pl.multiple_of(index * STEP, STEP), STEP)
            value = linear_term * x_next[rows, columns].astype(jnp.float32) + product(
                mixer[rows, :], x_next[:, columns], ((1,), (0,))
            )
            value = math.sqrt(WIDTH) * value.astype(jnp.bfloat16).astype(jnp.float32)
            value = jnp.where(active, value, 0.0)
            for row in range(LOCAL):
                for eight in range(SLOTS // 8):
                    for tile in range(STEP // LANES):
                        line = index * (STEP // LANES * LOCAL) + line_of(row, tile)
                        lines[eight, pl.ds(line, 8, stride=PITCH), :] = value[
                            row * SLOTS + eight * 8 : row * SLOTS + eight * 8 + 8, tile * LANES : (tile + 1) * LANES
                        ]
            return inner

        lax.fori_loop(0, WIDTH // STEP, columns_step, 0)

        def pack(eight, inner):
            pack_eight(lines.at[eight], sent, half * SLOTS + eight * 8)
            return inner

        lax.fori_loop(0, SLOTS // 8, pack, 0)
        return carry

    def give_back(index, carry):
        target = moved(index, -1)
        pltpu.make_async_remote_copy(
            src_ref=sent.at[index], dst_ref=returned.at[place], send_sem=back_out_sem,
            recv_sem=back_sems.at[place // GROUP], device_id=(target, core), device_id_type=MESH,
        ).start()
        return carry

    gone = sent.at[pl.ds(1, CHIPS - 1)]
    pltpu.make_async_copy(gone, gone, out_sem).wait()
    finish(0, 0)
    pltpu.make_async_copy(sent.at[0], returned.at[place], back_sems.at[place // GROUP]).start()
    lax.fori_loop(1, SLOTS, give_back, 0)
    finish(1, 0)
    lax.fori_loop(SLOTS, CHIPS, give_back, 0)

    def collect(group, carry):
        span = returned.at[pl.ds(group * GROUP, GROUP)]
        pltpu.make_async_copy(span, span, back_sems.at[group]).wait()
        for eight in range(2):
            unpack_eight(lines.at[eight], returned, group * GROUP + eight * 8)
        rows = pl.ds(pl.multiple_of(group * GROUP, GROUP), GROUP)
        for row in range(LOCAL):
            for tile in range(TILES):
                values = [read_lines(lines.at[eight], row, tile) for eight in range(2)]
                update[row, rows, tile * LANES : (tile + 1) * LANES] = jnp.concatenate(values, axis=0).astype(
                    jnp.bfloat16
                )
        return carry

    lax.fori_loop(0, GROUPS, collect, 0)
    pltpu.make_async_copy(gone, gone, back_out_sem).wait()


def on_device(momentum, gradient, assignment):
    shape = (LOCAL, CHIPS, WIDTH)
    blocks = pltpu.VMEM((CHIPS, *BLOCK), jnp.bfloat16)
    momentum_new, update = pl.pallas_call(
        kernel,
        out_shape=(
            jax.ShapeDtypeStruct(shape, jnp.float32),
            jax.ShapeDtypeStruct(shape, jnp.bfloat16),
        ),
        in_specs=[
            pl.BlockSpec(memory_space=pl.ANY),
            pl.BlockSpec(memory_space=pl.ANY),
            pl.BlockSpec(memory_space=pltpu.SMEM),
        ],
        out_specs=[pl.BlockSpec(memory_space=pltpu.VMEM)] * 2,
        scratch_shapes=[
            pltpu.VMEM((GROUPS, LOCAL, GROUP, WIDTH), jnp.float32),
            pltpu.VMEM((GROUPS, LOCAL, GROUP, WIDTH), jnp.bfloat16),
            blocks,
            blocks,
            blocks,
            pltpu.VMEM((ROWS, WIDTH), jnp.bfloat16),
            pltpu.VMEM((ROWS, WIDTH), jnp.bfloat16),
            pltpu.VMEM((ROWS, ROWS), jnp.float32),
            pltpu.VMEM((ROWS, ROWS), jnp.bfloat16),
            pltpu.VMEM((ROWS, ROWS), jnp.bfloat16),
            pltpu.VMEM((SLOTS // 8, 8 * PITCH, LANES), jnp.float32),
            pltpu.VMEM((8, LANES), jnp.float32),
            pltpu.VMEM((8, LANES), jnp.float32),
            pltpu.SemaphoreType.DMA((2, GROUPS)),
            pltpu.SemaphoreType.DMA,
            pltpu.SemaphoreType.DMA((GROUPS,)),
            pltpu.SemaphoreType.DMA,
            pltpu.SemaphoreType.DMA((GROUPS,)),
            pltpu.SemaphoreType.DMA,
            pltpu.SemaphoreType.DMA((1,)),
            pltpu.SemaphoreType.DMA((2,)),
        ],
        compiler_params=pltpu.CompilerParams(
            collective_id=0, has_side_effects=True, vmem_limit_bytes=56 * 2**20
        ),
        name="muon",
    )(jnp.transpose(momentum, (1, 0, 2)), jnp.transpose(gradient, (1, 0, 2)), assignment)
    return jnp.transpose(momentum_new, (1, 0, 2)), jnp.transpose(update, (1, 0, 2))


def solution(mesh):
    placed = P(None, ("dp", "tensor"), None)
    return jax.shard_map(
        on_device,
        mesh=mesh,
        in_specs=(placed, placed, P()),
        out_specs=(placed, placed),
        check_vma=False,
    )
```

```python
import functools
import math

import jax
import jax.numpy as jnp
from jax import lax
from jax.experimental import pallas as pl
from jax.experimental.pallas import tpu as pltpu
from jax.sharding import PartitionSpec as P

ITERS = 2
MESH = pl.DeviceIdType.MESH

momentum_rate = 0.95
epsilon_norm = 1e-07
linear_term = 3.4445
cubic_term = -4.775
quintic_term = 2.0315

SIDE = 4
CHIPS = SIDE**3
LOCAL = 6
WIDTH = 2560
LANES = 128
TILES = WIDTH // LANES
ROWS = LOCAL * CHIPS * 2
HALF = LOCAL * CHIPS
LINES = LOCAL * TILES
BLOCK = (8, LINES // 8 * LANES)
PITCH = LINES + 1
GROUP = 16
GROUPS = CHIPS // GROUP
SHARES = 4
SLOTS = CHIPS // SHARES
STEP = 512
TILE = 256
STRIPS = ROWS // TILE


def position():
    return lax.axis_index("dp"), lax.axis_index("tensor")


def spread_offsets():
    sets = []
    for offset in ((x, y, z) for x in range(SIDE) for y in range(SIDE) for z in range(SIDE)):
        turns = [offset[turn:] + offset[:turn] for turn in range(3)]
        alike = dict.fromkeys(tuple(sign * step % SIDE for step in turn) for sign in (1, -1) for turn in turns)
        if offset == min(alike):
            sets.append(list(alike))
    hops = [sum(min(step, SIDE - step) for step in alike[0]) for alike in sets]
    ranked = sorted(range(1, len(sets)), key=lambda index: -hops[index])
    return [offset for index in [0, *ranked] for offset in sets[index]]


OFFSETS = spread_offsets()


def targets(sign):
    place, _ = position()
    steps = []
    for scale in (SIDE * SIDE, SIDE, 1):
        here = place // scale % SIDE
        steps.append([(here + sign * away + SIDE) % SIDE * scale for away in range(SIDE)])
    return [steps[0][x] + steps[1][y] + steps[2][z] for x, y, z in OFFSETS]


def line_of(row, tile):
    return tile * LOCAL + row


def write_lines(scratch, row, tile, values):
    scratch[pl.ds(line_of(row, tile), 8, stride=PITCH), :] = values


def read_lines(scratch, row, tile):
    return scratch[pl.ds(line_of(row, tile), 8, stride=PITCH), :]


def pack_eight(scratch, blocks, first):
    for item in range(8):
        for part in range(LINES // 8):
            values = scratch[pl.ds(item * PITCH + 8 * part, 8), :]
            blocks[first + item, :, part * LANES : (part + 1) * LANES] = values.astype(jnp.bfloat16)


def unpack_eight(scratch, blocks, first):
    for item in range(8):
        values = blocks[first + item].astype(jnp.float32)
        for part in range(LINES // 8):
            scratch[pl.ds(item * PITCH + 8 * part, 8), :] = values[:, part * LANES : (part + 1) * LANES]


def product(a, b, dims):
    return lax.dot_general(a, b, (dims, ((), ())), preferred_element_type=jnp.float32)


def strip(index):
    return slice(index * TILE, (index + 1) * TILE)


def gram_of(x_ref, gram, low):
    for i in range(STRIPS):
        for j in range(i + 1):
            value = product(x_ref[strip(i), :], x_ref[strip(j), :], ((1,), (1,)))
            gram[strip(i), strip(j)] = value
            rounded = value.astype(jnp.bfloat16)
            low[strip(i), strip(j)] = rounded
            if i != j:
                low[strip(j), strip(i)] = value.T.astype(jnp.bfloat16)


def mixer_of(gram, low, mixer, j):
    for i in range(j, STRIPS):
        square = product(low[strip(i), :], low[:, strip(j)], ((1,), (0,)))
        value = cubic_term * gram[strip(i), strip(j)] + quintic_term * square
        mixer[strip(i), strip(j)] = value.astype(jnp.bfloat16)
        if i != j:
            mixer[strip(j), strip(i)] = value.T.astype(jnp.bfloat16)


def kernel(
    momentum, gradient, assignment, momentum_new, update,
    mom_in, grad_in, sent, arrived, returned, x_now, x_next, gram, low, mixer, lines, squares, squares_in,
    load_sems, out_sem, in_sems, back_out_sem, back_sems, pair_out_sem, pair_sems, square_sems,
):
    place, core = position()
    pair = (place, 1 - core)

    def load(group):
        rows = pl.ds(pl.multiple_of(group * GROUP, GROUP), GROUP)
        return (
            pltpu.make_async_copy(momentum.at[:, rows, :], mom_in.at[group], load_sems.at[0, group]),
            pltpu.make_async_copy(gradient.at[:, rows, :], grad_in.at[group], load_sems.at[1, group]),
        )

    for group in range(GROUPS):
        for copy in load(group):
            copy.start()

    barrier = pltpu.get_barrier_semaphore()
    pl.semaphore_signal(barrier, inc=1, device_id=pair, device_id_type=MESH)

    ahead = targets(1)
    for target in ahead[1:]:
        pl.semaphore_signal(barrier, inc=1, device_id=(target, core), device_id_type=MESH)

    def prepare(group, carry):
        for copy in load(group):
            copy.wait()
        rows = pl.ds(pl.multiple_of(group * GROUP, GROUP), GROUP)
        for row in range(LOCAL):
            for tile in range(TILES):
                columns = slice(tile * LANES, (tile + 1) * LANES)
                wide = grad_in[group, row, :, columns].astype(jnp.float32)
                fresh = momentum_rate * mom_in[group, row, :, columns] + wide
                momentum_new[row, rows, columns] = fresh
                direction = wide + momentum_rate * fresh
                for eight in range(2):
                    write_lines(lines.at[eight], row, tile, direction[eight * 8 : eight * 8 + 8])
        for eight in range(2):
            pack_eight(lines.at[eight], sent, group * GROUP + eight * 8)
        return carry

    lax.fori_loop(0, GROUPS, prepare, 0)

    pl.semaphore_wait(barrier, CHIPS)

    pltpu.make_async_copy(sent.at[place], arrived.at[0], in_sems.at[0]).start()

    for slot, target in enumerate(ahead):
        if slot:
            pltpu.make_async_remote_copy(
                src_ref=sent.at[target], dst_ref=arrived.at[slot], send_sem=out_sem, recv_sem=in_sems.at[slot // GROUP],
                device_id=(target, core), device_id_type=MESH,
            ).start()

    def rows_of(group, row):
        return pl.multiple_of(group * (LOCAL * GROUP) + row * GROUP, GROUP)

    def relay(group, row):
        start = rows_of(group, row)
        return pltpu.make_async_remote_copy(
            src_ref=x_now.at[pl.ds(start, GROUP), :], dst_ref=x_now.at[pl.ds(HALF + start, GROUP), :],
            send_sem=pair_out_sem, recv_sem=pair_sems.at[0], device_id=pair, device_id_type=MESH,
        )

    squares[...] = jnp.zeros_like(squares)

    def accept(group, carry):
        span = arrived.at[pl.ds(group * GROUP, GROUP)]
        pltpu.make_async_copy(span, span, in_sems.at[group]).wait()
        for eight in range(2):
            unpack_eight(lines.at[eight], arrived, group * GROUP + eight * 8)
        for row in range(LOCAL):
            start = rows_of(group, row)
            total = jnp.zeros((8, LANES), jnp.float32)
            for tile in range(TILES):
                values = [read_lines(lines.at[eight], row, tile) for eight in range(2)]
                for value in values:
                    total += value * value
                x_now[pl.ds(start, GROUP), tile * LANES : (tile + 1) * LANES] = jnp.concatenate(
                    values, axis=0
                ).astype(jnp.bfloat16)
            squares[...] += total
            relay(group, row).start()
        return carry

    lax.fori_loop(0, GROUPS, accept, 0)

    swap = pltpu.make_async_remote_copy(
        src_ref=squares, dst_ref=squares_in, send_sem=square_sems.at[0], recv_sem=square_sems.at[1],
        device_id=pair, device_id_type=MESH,
    )
    swap.start()
    swap.wait()
    own, other = x_now.at[pl.ds(0, HALF), :], x_now.at[pl.ds(HALF, HALF), :]
    pltpu.make_async_copy(own, own, pair_out_sem).wait()
    pltpu.make_async_copy(other, other, pair_sems.at[0]).wait()

    norm = jnp.sqrt(jnp.sum(squares[...] + squares_in[...])) + epsilon_norm

    def normalize(index, carry):
        rows = pl.ds(pl.multiple_of(index * 32, 32), 32)
        x_now[rows, :] = (x_now[rows, :].astype(jnp.float32) / norm).astype(jnp.bfloat16)
        return carry

    lax.fori_loop(0, ROWS // 32, normalize, 0)

    gram_of(x_now, gram, low)
    for j in range(STRIPS):
        mixer_of(gram, low, mixer, j)

    def mix(index, carry):
        columns = pl.ds(pl.multiple_of(index * STEP, STEP), STEP)
        for i in range(STRIPS):
            value = product(mixer[strip(i), :], x_now[:, columns], ((1,), (0,)))
            x_next[strip(i), columns] = (
                linear_term * x_now[strip(i), columns].astype(jnp.float32) + value
            ).astype(jnp.bfloat16)
        return carry

    lax.fori_loop(0, WIDTH // STEP, mix, 0)

    gram_of(x_next, gram, low)

    active = assignment[place] >= 0
    part = LOCAL * SLOTS

    def finish(share):
        rows = slice(share * part, (share + 1) * part)

        def columns_step(index, carry):
            columns = pl.ds(pl.multiple_of(index * STEP, STEP), STEP)
            value = linear_term * x_next[rows, columns].astype(jnp.float32) + product(
                mixer[rows, :], x_next[:, columns], ((1,), (0,))
            )
            value = math.sqrt(WIDTH) * value.astype(jnp.bfloat16).astype(jnp.float32)
            value = jnp.where(active, value, 0.0)
            for row in range(LOCAL):
                for eight in range(SLOTS // 8):
                    start = row * SLOTS + eight * 8
                    for tile in range(STEP // LANES):
                        line = index * (STEP // LANES * LOCAL) + line_of(row, tile)
                        lines[eight, pl.ds(line, 8, stride=PITCH), :] = value[
                            start : start + 8, tile * LANES : (tile + 1) * LANES
                        ]
            return carry

        lax.fori_loop(0, WIDTH // STEP, columns_step, 0)
        for eight in range(SLOTS // 8):
            pack_eight(lines.at[eight], sent, share * SLOTS + eight * 8)

    gone = sent.at[pl.ds(1, CHIPS - 1)]
    pltpu.make_async_copy(gone, gone, out_sem).wait()
    behind = targets(-1)
    for share in range(SHARES):
        for j in range(STRIPS):
            if share * part <= j * TILE < (share + 1) * part:
                mixer_of(gram, low, mixer, j)
        finish(share)
        for slot in range(share * SLOTS, (share + 1) * SLOTS):
            if slot == 0:
                pltpu.make_async_copy(sent.at[0], returned.at[place], back_sems.at[place // GROUP]).start()
            else:
                pltpu.make_async_remote_copy(
                    src_ref=sent.at[slot], dst_ref=returned.at[place], send_sem=back_out_sem,
                    recv_sem=back_sems.at[place // GROUP], device_id=(behind[slot], core), device_id_type=MESH,
                ).start()

    def collect(group, carry):
        span = returned.at[pl.ds(group * GROUP, GROUP)]
        pltpu.make_async_copy(span, span, back_sems.at[group]).wait()
        for eight in range(2):
            unpack_eight(lines.at[eight], returned, group * GROUP + eight * 8)
        rows = pl.ds(pl.multiple_of(group * GROUP, GROUP), GROUP)
        for row in range(LOCAL):
            for tile in range(TILES):
                values = [read_lines(lines.at[eight], row, tile) for eight in range(2)]
                update[row, rows, tile * LANES : (tile + 1) * LANES] = jnp.concatenate(values, axis=0).astype(
                    jnp.bfloat16
                )
        return carry

    lax.fori_loop(0, GROUPS, collect, 0)
    pltpu.make_async_copy(gone, gone, back_out_sem).wait()


def on_device(momentum, gradient, assignment):
    shape = (LOCAL, CHIPS, WIDTH)
    blocks = pltpu.VMEM((CHIPS, *BLOCK), jnp.bfloat16)
    momentum_new, update = pl.pallas_call(
        kernel,
        out_shape=(
            pltpu.VMEM(shape, jnp.float32),
            pltpu.VMEM(shape, jnp.bfloat16),
        ),
        in_specs=[
            pl.BlockSpec(memory_space=pl.ANY),
            pl.BlockSpec(memory_space=pl.ANY),
            pl.BlockSpec(memory_space=pltpu.SMEM),
        ],
        out_specs=[pl.BlockSpec(memory_space=pltpu.VMEM)] * 2,
        scratch_shapes=[
            pltpu.VMEM((GROUPS, LOCAL, GROUP, WIDTH), jnp.float32),
            pltpu.VMEM((GROUPS, LOCAL, GROUP, WIDTH), jnp.bfloat16),
            blocks,
            blocks,
            blocks,
            pltpu.VMEM((ROWS, WIDTH), jnp.bfloat16),
            pltpu.VMEM((ROWS, WIDTH), jnp.bfloat16),
            pltpu.VMEM((ROWS, ROWS), jnp.float32),
            pltpu.VMEM((ROWS, ROWS), jnp.bfloat16),
            pltpu.VMEM((ROWS, ROWS), jnp.bfloat16),
            pltpu.VMEM((SLOTS // 8, 8 * PITCH, LANES), jnp.float32),
            pltpu.VMEM((8, LANES), jnp.float32),
            pltpu.VMEM((8, LANES), jnp.float32),
            pltpu.SemaphoreType.DMA((2, GROUPS)),
            pltpu.SemaphoreType.DMA,
            pltpu.SemaphoreType.DMA((GROUPS,)),
            pltpu.SemaphoreType.DMA,
            pltpu.SemaphoreType.DMA((GROUPS,)),
            pltpu.SemaphoreType.DMA,
            pltpu.SemaphoreType.DMA((1,)),
            pltpu.SemaphoreType.DMA((2,)),
        ],
        compiler_params=pltpu.CompilerParams(
            collective_id=0, has_side_effects=True, vmem_limit_bytes=56 * 2**20
        ),
        name="muon",
    )(jnp.transpose(momentum, (1, 0, 2)), jnp.transpose(gradient, (1, 0, 2)), assignment)
    return jnp.transpose(momentum_new, (1, 0, 2)), jnp.transpose(update, (1, 0, 2))


def solution(mesh):
    placed = P(None, ("dp", "tensor"), None)
    return jax.shard_map(
        on_device,
        mesh=mesh,
        in_specs=(placed, placed, P()),
        out_specs=(placed, placed),
        check_vma=False,
    )
```

```python
import math

import jax
import jax.numpy as jnp
from jax import lax
from jax.experimental import pallas as pl
from jax.experimental.pallas import tpu as pltpu
from jax.sharding import PartitionSpec as P

ITERS = 2
MESH = pl.DeviceIdType.MESH

momentum_rate = 0.95
epsilon_norm = 1e-07
linear_term = 3.4445
cubic_term = -4.775
quintic_term = 2.0315

SIDE = 4
CHIPS = SIDE**3
LOCAL = 6
WIDTH = 2560
LANES = 128
TILES = WIDTH // LANES
ROWS = LOCAL * CHIPS * 2
HALF = LOCAL * CHIPS
LINES = LOCAL * TILES
BLOCK = (8, LINES // 8 * LANES)
PITCH = LINES + 1
GROUP = 16
GROUPS = CHIPS // GROUP
PIECE = 4
PIECES = CHIPS // PIECE
SHARES = ((0, 1), (1, GROUPS))
TILE = 256
STRIPS = ROWS // TILE


def position():
    return lax.axis_index("dp"), lax.axis_index("tensor")


def spread_offsets():
    sets = []
    for offset in ((x, y, z) for x in range(SIDE) for y in range(SIDE) for z in range(SIDE)):
        turns = [offset[turn:] + offset[:turn] for turn in range(3)]
        alike = dict.fromkeys(tuple(sign * step % SIDE for step in turn) for sign in (1, -1) for turn in turns)
        if offset == min(alike):
            sets.append(list(alike))
    hops = [sum(min(step, SIDE - step) for step in alike[0]) for alike in sets]
    ranked = sorted(range(1, len(sets)), key=lambda index: -hops[index])
    return [offset for index in [0, *ranked] for offset in sets[index]]


OFFSETS = spread_offsets()


def targets(sign):
    place, _ = position()
    steps = []
    for scale in (SIDE * SIDE, SIDE, 1):
        here = place // scale % SIDE
        steps.append([(here + sign * away + SIDE) % SIDE * scale for away in range(SIDE)])
    return [steps[0][x] + steps[1][y] + steps[2][z] for x, y, z in OFFSETS]


def line_of(row, tile):
    return tile * LOCAL + row


def write_lines(scratch, row, tile, values):
    scratch[pl.ds(line_of(row, tile), 8, stride=PITCH), :] = values


def read_lines(scratch, row, tile):
    return scratch[pl.ds(line_of(row, tile), 8, stride=PITCH), :]


def pack_eight(scratch, blocks, first):
    for item in range(8):
        for part in range(LINES // 8):
            values = scratch[pl.ds(item * PITCH + 8 * part, 8), :]
            blocks[first + item, :, part * LANES : (part + 1) * LANES] = values.astype(jnp.bfloat16)


def unpack_eight(scratch, blocks, first):
    for item in range(8):
        values = blocks[first + item].astype(jnp.float32)
        for part in range(LINES // 8):
            scratch[pl.ds(item * PITCH + 8 * part, 8), :] = values[:, part * LANES : (part + 1) * LANES]


def product(a, b, dims):
    return lax.dot_general(a, b, (dims, ((), ())), preferred_element_type=jnp.float32)


def strip(index):
    return slice(index * TILE, (index + 1) * TILE)


def gram_block(x_ref, i, j):
    return product(x_ref[strip(i), :], x_ref[strip(j), :], ((1,), (1,)))


def keep_block(gram, low, i, j, value):
    gram[strip(i), strip(j)] = value
    low[strip(i), strip(j)] = value.astype(jnp.bfloat16)
    if i != j:
        low[strip(j), strip(i)] = value.T.astype(jnp.bfloat16)


def lay_out(lines, blocks, group, write):
    for eight in range(2):
        unpack_eight(lines.at[eight], blocks, group * GROUP + eight * 8)
    for row in range(LOCAL):
        for tile in range(TILES):
            values = [read_lines(lines.at[eight], row, tile) for eight in range(2)]
            write(row, tile, jnp.concatenate(values, axis=0).astype(jnp.bfloat16))


def share_rows(group, core=0):
    return (2 * group + core) * LOCAL * GROUP


def mixer_of(gram, low, mixer, j):
    for i in range(j, STRIPS):
        square = product(low[strip(i), :], low[:, strip(j)], ((1,), (0,)))
        value = cubic_term * gram[strip(i), strip(j)] + quintic_term * square
        mixer[strip(i), strip(j)] = value.astype(jnp.bfloat16)
        if i != j:
            mixer[strip(j), strip(i)] = value.T.astype(jnp.bfloat16)


def kernel(
    momentum, gradient, assignment, momentum_new, returned,
    mom_in, grad_in, sent, arrived, relayed, x_now, x_next, gram, low, mixer, lines,
    load_sems, out_sem, in_sems, back_out_sem, back_sem, pair_out_sem, pair_sems,
):
    place, core = position()
    pair = (place, 1 - core)

    def load(group):
        rows = pl.ds(pl.multiple_of(group * GROUP, GROUP), GROUP)
        return (
            pltpu.make_async_copy(momentum.at[:, rows, :], mom_in.at[group], load_sems.at[0, group]),
            pltpu.make_async_copy(gradient.at[:, rows, :], grad_in.at[group], load_sems.at[1, group]),
        )

    for group in range(GROUPS):
        for copy in load(group):
            copy.start()

    barrier = pltpu.get_barrier_semaphore()
    pl.semaphore_signal(barrier, inc=1, device_id=pair, device_id_type=MESH)

    ahead = targets(1)
    for target in ahead[1:]:
        pl.semaphore_signal(barrier, inc=1, device_id=(target, core), device_id_type=MESH)

    def prepare(group, carry):
        for copy in load(group):
            copy.wait()
        rows = pl.ds(pl.multiple_of(group * GROUP, GROUP), GROUP)
        for row in range(LOCAL):
            for tile in range(TILES):
                columns = slice(tile * LANES, (tile + 1) * LANES)
                wide = grad_in[group, row, :, columns].astype(jnp.float32)
                fresh = momentum_rate * mom_in[group, row, :, columns] + wide
                momentum_new[row, rows, columns] = fresh
                direction = wide + momentum_rate * fresh
                for eight in range(2):
                    write_lines(lines.at[eight], row, tile, direction[eight * 8 : eight * 8 + 8])
        for eight in range(2):
            pack_eight(lines.at[eight], sent, group * GROUP + eight * 8)
        return carry

    lax.fori_loop(0, GROUPS, prepare, 0)

    pl.semaphore_wait(barrier, CHIPS)

    pltpu.make_async_copy(sent.at[place], arrived.at[0], in_sems.at[0]).start()

    for slot, target in enumerate(ahead):
        if slot:
            pltpu.make_async_remote_copy(
                src_ref=sent.at[target], dst_ref=arrived.at[slot], send_sem=out_sem, recv_sem=in_sems.at[slot // PIECE],
                device_id=(target, core), device_id_type=MESH,
            ).start()

    def accept(blocks, group, which):
        def write(row, tile, values):
            start = share_rows(group, which) + row * GROUP
            x_now[start : start + GROUP, tile * LANES : (tile + 1) * LANES] = values

        lay_out(lines, blocks, group, write)

    def accept_pair(group):
        span = relayed.at[pl.ds(group * GROUP, GROUP)]
        pltpu.make_async_copy(span, span, pair_sems.at[group]).wait()
        accept(relayed, group, 1)
        for i in range(STRIPS):
            if share_rows(group) < (i + 1) * TILE <= share_rows(group + 1):
                for j in range(i + 1):
                    gram[strip(i), strip(j)] = gram_block(x_now, i, j)

    for group in range(GROUPS):
        if group:
            accept_pair(group - 1)
        for piece in range(group * GROUP // PIECE, (group + 1) * GROUP // PIECE):
            span = pl.ds(piece * PIECE, PIECE)
            pltpu.make_async_copy(arrived.at[span], arrived.at[span], in_sems.at[piece]).wait()
            pltpu.make_async_remote_copy(
                src_ref=arrived.at[span], dst_ref=relayed.at[span], send_sem=pair_out_sem, recv_sem=pair_sems.at[group],
                device_id=pair, device_id_type=MESH,
            ).start()
        accept(arrived, group, 0)
    accept_pair(GROUPS - 1)

    diagonal = lax.broadcasted_iota(jnp.int32, (TILE, TILE), 0) == lax.broadcasted_iota(jnp.int32, (TILE, TILE), 1)
    total = jnp.zeros((TILE, TILE), jnp.float32)
    for i in range(STRIPS):
        total += jnp.where(diagonal, gram[strip(i), strip(i)], 0.0)
    total = jnp.sum(total)
    scale = 1.0 / (jnp.sqrt(total) + epsilon_norm)
    for i in range(STRIPS):
        for j in range(i + 1):
            value = jnp.where(scale > 0.0, gram[strip(i), strip(j)] * scale * scale, 0.0)
            keep_block(gram, low, i, j, value)

    def normalize(part):
        rows = slice(part * LANES, (part + 1) * LANES)
        x_now[rows, :] = (x_now[rows, :].astype(jnp.float32) * scale).astype(jnp.bfloat16)

    for j in range(STRIPS):
        mixer_of(gram, low, mixer, j)
        normalize(2 * j)
        normalize(2 * j + 1)

    for i in range(STRIPS):
        value = product(mixer[strip(i), :], x_now[...], ((1,), (0,)))
        x_next[strip(i), :] = (linear_term * x_now[strip(i), :].astype(jnp.float32) + value).astype(jnp.bfloat16)

    for i in range(STRIPS):
        for j in range(i + 1):
            keep_block(gram, low, i, j, gram_block(x_next, i, j))

    active = assignment[place] >= 0
    made = set()

    def finish(first, last):
        for group in range(first, last):
            for j in range(STRIPS):
                if j not in made and share_rows(group) < (j + 1) * TILE and j * TILE < share_rows(group, 1):
                    made.add(j)
                    mixer_of(gram, low, mixer, j)
        rows = [slice(share_rows(group), share_rows(group, 1)) for group in range(first, last)]

        def gathered(ref):
            parts = [ref[row, :] for row in rows]
            return parts[0] if len(parts) == 1 else jnp.concatenate(parts, axis=0)

        value = linear_term * gathered(x_next).astype(jnp.float32) + product(
            gathered(mixer), x_next[...], ((1,), (0,))
        )
        value = math.sqrt(WIDTH) * value.astype(jnp.bfloat16).astype(jnp.float32)
        value = jnp.where(active, value, 0.0)
        for group in range(first, last):
            for eight in range(2):
                place_lines = lines.at[2 * (group - first) + eight]
                for row in range(LOCAL):
                    start = (group - first) * LOCAL * GROUP + row * GROUP + eight * 8
                    for tile in range(TILES):
                        write_lines(
                            place_lines, row, tile, value[start : start + 8, tile * LANES : (tile + 1) * LANES]
                        )
                pack_eight(place_lines, sent, group * GROUP + eight * 8)

    gone = sent.at[pl.ds(1, CHIPS - 1)]
    pltpu.make_async_copy(gone, gone, out_sem).wait()
    behind = targets(-1)
    for first, last in SHARES:
        finish(first, last)
        for slot in range(first * GROUP, last * GROUP):
            if slot == 0:
                pltpu.make_async_copy(sent.at[0], returned.at[place], back_sem).start()
            else:
                pltpu.make_async_remote_copy(
                    src_ref=sent.at[slot], dst_ref=returned.at[place], send_sem=back_out_sem, recv_sem=back_sem,
                    device_id=(behind[slot], core), device_id_type=MESH,
                ).start()

    pltpu.make_async_copy(arrived, arrived, pair_out_sem).wait()
    pltpu.make_async_copy(returned, returned, back_sem).wait()
    pltpu.make_async_copy(gone, gone, back_out_sem).wait()


def place_results(fresh, returned, momentum_new, update, rows_out, lines, fresh_sem, group_sems):
    whole = pltpu.make_async_copy(fresh, momentum_new, fresh_sem)
    whole.start()
    copies = []
    for group in range(GROUPS):
        rows = pl.ds(group * GROUP, GROUP)

        def write(row, tile, values):
            rows_out[row, group * GROUP : (group + 1) * GROUP, tile * LANES : (tile + 1) * LANES] = values

        lay_out(lines, returned, group, write)
        copies.append(
            pltpu.make_async_copy(rows_out.at[:, rows, :], update.at[:, rows, :], group_sems.at[group])
        )
        copies[-1].start()
    for copy in copies:
        copy.wait()
    whole.wait()


def on_device(momentum, gradient, assignment):
    shape = (LOCAL, CHIPS, WIDTH)
    blocks = pltpu.VMEM((CHIPS, *BLOCK), jnp.bfloat16)
    line_space = pltpu.VMEM((2 * GROUPS, 8 * PITCH, LANES), jnp.float32)
    fresh, returned = pl.pallas_call(
        kernel,
        out_shape=(pltpu.VMEM(shape, jnp.float32), blocks),
        in_specs=[
            pl.BlockSpec(memory_space=pl.ANY),
            pl.BlockSpec(memory_space=pl.ANY),
            pl.BlockSpec(memory_space=pltpu.SMEM),
        ],
        out_specs=[pl.BlockSpec(memory_space=pltpu.VMEM)] * 2,
        scratch_shapes=[
            pltpu.VMEM((GROUPS, LOCAL, GROUP, WIDTH), jnp.float32),
            pltpu.VMEM((GROUPS, LOCAL, GROUP, WIDTH), jnp.bfloat16),
            blocks,
            blocks,
            blocks,
            pltpu.VMEM((ROWS, WIDTH), jnp.bfloat16),
            pltpu.VMEM((ROWS, WIDTH), jnp.bfloat16),
            pltpu.VMEM((ROWS, ROWS), jnp.float32),
            pltpu.VMEM((ROWS, ROWS), jnp.bfloat16),
            pltpu.VMEM((ROWS, ROWS), jnp.bfloat16),
            line_space,
            pltpu.SemaphoreType.DMA((2, GROUPS)),
            pltpu.SemaphoreType.DMA,
            pltpu.SemaphoreType.DMA((PIECES,)),
            pltpu.SemaphoreType.DMA,
            pltpu.SemaphoreType.DMA,
            pltpu.SemaphoreType.DMA,
            pltpu.SemaphoreType.DMA((GROUPS,)),
        ],
        compiler_params=pltpu.CompilerParams(
            collective_id=0, has_side_effects=True, vmem_limit_bytes=50 * 2**20
        ),
        name="muon",
    )(jnp.transpose(momentum, (1, 0, 2)), jnp.transpose(gradient, (1, 0, 2)), assignment)
    momentum_new, update = pl.pallas_call(
        place_results,
        out_shape=(jax.ShapeDtypeStruct(shape, jnp.float32), jax.ShapeDtypeStruct(shape, jnp.bfloat16)),
        in_specs=[pl.BlockSpec(memory_space=pltpu.VMEM)] * 2,
        out_specs=[pl.BlockSpec(memory_space=pl.ANY)] * 2,
        scratch_shapes=[
            pltpu.VMEM(shape, jnp.bfloat16),
            line_space,
            pltpu.SemaphoreType.DMA,
            pltpu.SemaphoreType.DMA((GROUPS,)),
        ],
        compiler_params=pltpu.CompilerParams(vmem_limit_bytes=32 * 2**20),
        name="place_results",
    )(fresh, returned)
    return jnp.transpose(momentum_new, (1, 0, 2)), jnp.transpose(update, (1, 0, 2))


def solution(mesh):
    placed = P(None, ("dp", "tensor"), None)
    return jax.shard_map(
        on_device,
        mesh=mesh,
        in_specs=(placed, placed, P()),
        out_specs=(placed, placed),
        check_vma=False,
    )
```

```python
import math

import jax
import jax.numpy as jnp
from jax import lax
from jax.experimental import pallas as pl
from jax.experimental.pallas import tpu as pltpu
from jax.sharding import PartitionSpec as P

ITERS = 2
MESH = pl.DeviceIdType.MESH

momentum_rate = 0.95
epsilon_norm = 1e-07
linear_term = 3.4445
cubic_term = -4.775
quintic_term = 2.0315

SIDE = 4
CHIPS = SIDE**3
LOCAL = 6
WIDTH = 2560
LANES = 128
TILES = WIDTH // LANES
ROWS = LOCAL * CHIPS * 2
HALF = LOCAL * CHIPS
LINES = LOCAL * TILES
BLOCK = (8, LINES // 8 * LANES)
PITCH = LINES + 1
GROUP = 16
GROUPS = CHIPS // GROUP
PIECE = 4
PIECES = CHIPS // PIECE
SHARES = ((0, 1), (1, GROUPS))
TILE = 256
STRIPS = ROWS // TILE


def position():
    return lax.axis_index("dp"), lax.axis_index("tensor")


def spread_offsets():
    sets = []
    for offset in ((x, y, z) for x in range(SIDE) for y in range(SIDE) for z in range(SIDE)):
        turns = [offset[turn:] + offset[:turn] for turn in range(3)]
        alike = dict.fromkeys(tuple(sign * step % SIDE for step in turn) for sign in (1, -1) for turn in turns)
        if offset == min(alike):
            sets.append(list(alike))
    hops = [sum(min(step, SIDE - step) for step in alike[0]) for alike in sets]
    ranked, rest = [], {}
    for index in range(1, len(sets)):
        rest.setdefault(hops[index], []).append(index)
    while any(rest.values()):
        for some in rest.values():
            if some:
                ranked.append(some.pop())
    return [offset for index in [0, *ranked] for offset in sets[index]]


OFFSETS = spread_offsets()


def targets(sign):
    place, _ = position()
    steps = []
    for scale in (SIDE * SIDE, SIDE, 1):
        here = place // scale % SIDE
        steps.append([(here + sign * away + SIDE) % SIDE * scale for away in range(SIDE)])
    return [steps[0][x] + steps[1][y] + steps[2][z] for x, y, z in OFFSETS]


def line_of(row, tile):
    return tile * LOCAL + row


def write_lines(scratch, row, tile, values):
    scratch[pl.ds(line_of(row, tile), 8, stride=PITCH), :] = values


def read_lines(scratch, row, tile):
    return scratch[pl.ds(line_of(row, tile), 8, stride=PITCH), :]


def pack_eight(scratch, blocks, first):
    for item in range(8):
        for part in range(LINES // 8):
            values = scratch[pl.ds(item * PITCH + 8 * part, 8), :]
            blocks[first + item, :, part * LANES : (part + 1) * LANES] = values.astype(jnp.bfloat16)


def unpack_eight(scratch, blocks, first):
    for item in range(8):
        values = blocks[first + item].astype(jnp.float32)
        for part in range(LINES // 8):
            scratch[pl.ds(item * PITCH + 8 * part, 8), :] = values[:, part * LANES : (part + 1) * LANES]


def product(a, b, dims):
    return lax.dot_general(a, b, (dims, ((), ())), preferred_element_type=jnp.float32)


def strip(index):
    return slice(index * TILE, (index + 1) * TILE)


def gram_block(x_ref, i, j):
    return product(x_ref[strip(i), :], x_ref[strip(j), :], ((1,), (1,)))


def keep_block(gram, low, i, j, value):
    gram[strip(i), strip(j)] = value
    low[strip(i), strip(j)] = value.astype(jnp.bfloat16)
    if i != j:
        low[strip(j), strip(i)] = value.T.astype(jnp.bfloat16)


def lay_out(lines, blocks, group, write, sums=None):
    for eight in range(2):
        unpack_eight(lines.at[eight], blocks, group * GROUP + eight * 8)
    for row in range(LOCAL):
        for tile in range(TILES):
            values = [read_lines(lines.at[eight], row, tile) for eight in range(2)]
            write(row, tile, jnp.concatenate(values, axis=0).astype(jnp.bfloat16))
            for index, value in enumerate(values if sums else ()):
                sums[2 * (tile % 2) + index] += value * value


def share_rows(group, core=0):
    return (2 * group + core) * LOCAL * GROUP


def mixer_of(gram, low, mixer, j):
    for i in range(j, STRIPS):
        square = product(low[strip(i), :], low[:, strip(j)], ((1,), (0,)))
        value = cubic_term * gram[strip(i), strip(j)] + quintic_term * square
        mixer[strip(i), strip(j)] = value.astype(jnp.bfloat16)
        if i != j:
            mixer[strip(j), strip(i)] = value.T.astype(jnp.bfloat16)


def kernel(
    momentum, gradient, assignment, momentum_new, returned,
    mom_in, grad_in, sent, arrived, relayed, x_now, x_next, gram, low, mixer, lines, squares,
    load_sems, out_sem, in_sems, back_out_sem, back_sem, pair_out_sem, pair_sems,
):
    place, core = position()
    pair = (place, 1 - core)

    def load(group):
        rows = pl.ds(pl.multiple_of(group * GROUP, GROUP), GROUP)
        return (
            pltpu.make_async_copy(momentum.at[:, rows, :], mom_in.at[group], load_sems.at[0, group]),
            pltpu.make_async_copy(gradient.at[:, rows, :], grad_in.at[group], load_sems.at[1, group]),
        )

    for group in range(GROUPS):
        for copy in load(group):
            copy.start()

    barrier = pltpu.get_barrier_semaphore()
    pl.semaphore_signal(barrier, inc=1, device_id=pair, device_id_type=MESH)

    ahead = targets(1)
    for target in ahead[1:]:
        pl.semaphore_signal(barrier, inc=1, device_id=(target, core), device_id_type=MESH)

    def prepare(group, carry):
        for copy in load(group):
            copy.wait()
        rows = pl.ds(pl.multiple_of(group * GROUP, GROUP), GROUP)
        for row in range(LOCAL):
            for tile in range(TILES):
                columns = slice(tile * LANES, (tile + 1) * LANES)
                wide = grad_in[group, row, :, columns].astype(jnp.float32)
                fresh = momentum_rate * mom_in[group, row, :, columns] + wide
                momentum_new[row, rows, columns] = fresh
                direction = wide + momentum_rate * fresh
                for eight in range(2):
                    write_lines(lines.at[eight], row, tile, direction[eight * 8 : eight * 8 + 8])
        for eight in range(2):
            pack_eight(lines.at[eight], sent, group * GROUP + eight * 8)
        return carry

    lax.fori_loop(0, GROUPS, prepare, 0)

    pl.semaphore_wait(barrier, CHIPS)

    pltpu.make_async_copy(sent.at[place], arrived.at[0], in_sems.at[0]).start()

    for slot, target in enumerate(ahead):
        if slot:
            pltpu.make_async_remote_copy(
                src_ref=sent.at[target], dst_ref=arrived.at[slot], send_sem=out_sem, recv_sem=in_sems.at[slot // PIECE],
                device_id=(target, core), device_id_type=MESH,
            ).start()

    def accept(blocks, group, which):
        def write(row, tile, values):
            start = share_rows(group, which) + row * GROUP
            x_now[start : start + GROUP, tile * LANES : (tile + 1) * LANES] = values

        sums = [jnp.zeros((8, LANES), jnp.float32)] * 4
        lay_out(lines, blocks, group, write, sums)
        squares[...] += (sums[0] + sums[1]) + (sums[2] + sums[3])

    def accept_pair(group):
        span = relayed.at[pl.ds(group * GROUP, GROUP)]
        pltpu.make_async_copy(span, span, pair_sems.at[group]).wait()
        accept(relayed, group, 1)
        for i in range(STRIPS - 1):
            if share_rows(group) < (i + 1) * TILE <= share_rows(group + 1):
                for j in range(i + 1):
                    gram[strip(i), strip(j)] = gram_block(x_now, i, j)

    squares[...] = jnp.zeros_like(squares)
    for group in range(GROUPS):
        if group:
            accept_pair(group - 1)
        for piece in range(group * GROUP // PIECE, (group + 1) * GROUP // PIECE):
            span = pl.ds(piece * PIECE, PIECE)
            pltpu.make_async_copy(arrived.at[span], arrived.at[span], in_sems.at[piece]).wait()
            pltpu.make_async_remote_copy(
                src_ref=arrived.at[span], dst_ref=relayed.at[span], send_sem=pair_out_sem, recv_sem=pair_sems.at[group],
                device_id=pair, device_id_type=MESH,
            ).start()
        accept(arrived, group, 0)
    accept_pair(GROUPS - 1)

    scale = 1.0 / (jnp.sqrt(jnp.sum(squares[...])) + epsilon_norm)

    def scaled(value):
        return jnp.where(scale > 0.0, value * scale * scale, 0.0)

    before = [(i, j) for i in range(STRIPS - 1) for j in range(i + 1)]
    for j in range(STRIPS):
        keep_block(gram, low, STRIPS - 1, j, scaled(gram_block(x_now, STRIPS - 1, j)))
        for i, k in before[j::STRIPS]:
            keep_block(gram, low, i, k, scaled(gram[strip(i), strip(k)]))

    for j in range(STRIPS):
        mixer_of(gram, low, mixer, j)

    for index in range(WIDTH // TILE):
        start = (x_now[:, strip(index)].astype(jnp.float32) * scale).astype(jnp.bfloat16)
        value = product(mixer[...], start, ((1,), (0,)))
        x_next[:, strip(index)] = (linear_term * start.astype(jnp.float32) + value).astype(jnp.bfloat16)

    for i in range(STRIPS):
        for j in range(i + 1):
            keep_block(gram, low, i, j, gram_block(x_next, i, j))

    active = assignment[place] >= 0
    made = set()

    def finish(first, last):
        for group in range(first, last):
            for j in range(STRIPS):
                if j not in made and share_rows(group) < (j + 1) * TILE and j * TILE < share_rows(group, 1):
                    made.add(j)
                    mixer_of(gram, low, mixer, j)
        rows = [slice(share_rows(group), share_rows(group, 1)) for group in range(first, last)]

        def gathered(ref):
            parts = [ref[row, :] for row in rows]
            return parts[0] if len(parts) == 1 else jnp.concatenate(parts, axis=0)

        value = linear_term * gathered(x_next).astype(jnp.float32) + product(
            gathered(mixer), x_next[...], ((1,), (0,))
        )
        value = math.sqrt(WIDTH) * value.astype(jnp.bfloat16).astype(jnp.float32)
        value = jnp.where(active, value, 0.0)
        for group in range(first, last):
            for eight in range(2):
                place_lines = lines.at[2 * (group - first) + eight]
                for row in range(LOCAL):
                    start = (group - first) * LOCAL * GROUP + row * GROUP + eight * 8
                    for tile in range(TILES):
                        write_lines(
                            place_lines, row, tile, value[start : start + 8, tile * LANES : (tile + 1) * LANES]
                        )
                pack_eight(place_lines, sent, group * GROUP + eight * 8)

    gone = sent.at[pl.ds(1, CHIPS - 1)]
    pltpu.make_async_copy(gone, gone, out_sem).wait()
    behind = targets(-1)
    for first, last in SHARES:
        finish(first, last)
        for slot in range(first * GROUP, last * GROUP):
            if slot == 0:
                pltpu.make_async_copy(sent.at[0], returned.at[place], back_sem).start()
            else:
                pltpu.make_async_remote_copy(
                    src_ref=sent.at[slot], dst_ref=returned.at[place], send_sem=back_out_sem, recv_sem=back_sem,
                    device_id=(behind[slot], core), device_id_type=MESH,
                ).start()

    pltpu.make_async_copy(arrived, arrived, pair_out_sem).wait()
    pltpu.make_async_copy(returned, returned, back_sem).wait()
    pltpu.make_async_copy(gone, gone, back_out_sem).wait()


def place_results(fresh, returned, momentum_new, update, rows_out, lines, fresh_sem, group_sems):
    whole = pltpu.make_async_copy(fresh, momentum_new, fresh_sem)
    whole.start()
    copies = []
    for group in range(GROUPS):
        rows = pl.ds(group * GROUP, GROUP)

        def write(row, tile, values):
            rows_out[row, group * GROUP : (group + 1) * GROUP, tile * LANES : (tile + 1) * LANES] = values

        lay_out(lines, returned, group, write)
        copies.append(
            pltpu.make_async_copy(rows_out.at[:, rows, :], update.at[:, rows, :], group_sems.at[group])
        )
        copies[-1].start()
    for copy in copies:
        copy.wait()
    whole.wait()


def on_device(momentum, gradient, assignment):
    shape = (LOCAL, CHIPS, WIDTH)
    blocks = pltpu.VMEM((CHIPS, *BLOCK), jnp.bfloat16)
    line_space = pltpu.VMEM((2 * GROUPS, 8 * PITCH, LANES), jnp.float32)
    fresh, returned = pl.pallas_call(
        kernel,
        out_shape=(pltpu.VMEM(shape, jnp.float32), blocks),
        in_specs=[
            pl.BlockSpec(memory_space=pl.ANY),
            pl.BlockSpec(memory_space=pl.ANY),
            pl.BlockSpec(memory_space=pltpu.SMEM),
        ],
        out_specs=[pl.BlockSpec(memory_space=pltpu.VMEM)] * 2,
        scratch_shapes=[
            pltpu.VMEM((GROUPS, LOCAL, GROUP, WIDTH), jnp.float32),
            pltpu.VMEM((GROUPS, LOCAL, GROUP, WIDTH), jnp.bfloat16),
            blocks,
            blocks,
            blocks,
            pltpu.VMEM((ROWS, WIDTH), jnp.bfloat16),
            pltpu.VMEM((ROWS, WIDTH), jnp.bfloat16),
            pltpu.VMEM((ROWS, ROWS), jnp.float32),
            pltpu.VMEM((ROWS, ROWS), jnp.bfloat16),
            pltpu.VMEM((ROWS, ROWS), jnp.bfloat16),
            line_space,
            pltpu.VMEM((8, LANES), jnp.float32),
            pltpu.SemaphoreType.DMA((2, GROUPS)),
            pltpu.SemaphoreType.DMA,
            pltpu.SemaphoreType.DMA((PIECES,)),
            pltpu.SemaphoreType.DMA,
            pltpu.SemaphoreType.DMA,
            pltpu.SemaphoreType.DMA,
            pltpu.SemaphoreType.DMA((GROUPS,)),
        ],
        compiler_params=pltpu.CompilerParams(
            collective_id=0, has_side_effects=True, vmem_limit_bytes=50 * 2**20
        ),
        name="muon",
    )(jnp.transpose(momentum, (1, 0, 2)), jnp.transpose(gradient, (1, 0, 2)), assignment)
    momentum_new, update = pl.pallas_call(
        place_results,
        out_shape=(jax.ShapeDtypeStruct(shape, jnp.float32), jax.ShapeDtypeStruct(shape, jnp.bfloat16)),
        in_specs=[pl.BlockSpec(memory_space=pltpu.VMEM)] * 2,
        out_specs=[pl.BlockSpec(memory_space=pl.ANY)] * 2,
        scratch_shapes=[
            pltpu.VMEM(shape, jnp.bfloat16),
            line_space,
            pltpu.SemaphoreType.DMA,
            pltpu.SemaphoreType.DMA((GROUPS,)),
        ],
        compiler_params=pltpu.CompilerParams(vmem_limit_bytes=32 * 2**20),
        name="place_results",
    )(fresh, returned)
    return jnp.transpose(momentum_new, (1, 0, 2)), jnp.transpose(update, (1, 0, 2))


def solution(mesh):
    placed = P(None, ("dp", "tensor"), None)
    return jax.shard_map(
        on_device,
        mesh=mesh,
        in_specs=(placed, placed, P()),
        out_specs=(placed, placed),
        check_vma=False,
    )
```

```python
import math

import jax
import jax.numpy as jnp
from jax import lax
from jax.experimental import pallas as pl
from jax.experimental.pallas import tpu as pltpu
from jax.sharding import PartitionSpec as P

ITERS = 2
MESH = pl.DeviceIdType.MESH

momentum_rate = 0.95
epsilon_norm = 1e-07
linear_term = 3.4445
cubic_term = -4.775
quintic_term = 2.0315

SIDE = 4
CHIPS = SIDE**3
LOCAL = 6
WIDTH = 2560
LANES = 128
TILES = WIDTH // LANES
ROWS = LOCAL * CHIPS * 2
HALF = LOCAL * CHIPS
LINES = LOCAL * TILES
BLOCK = (8, LINES // 8 * LANES)
PITCH = LINES + 1
GROUP = 16
GROUPS = CHIPS // GROUP
PIECE = 4
PIECES = CHIPS // PIECE
SHARES = ((0, 1), (1, GROUPS))
TILE = 256
STRIPS = ROWS // TILE


def position():
    return lax.axis_index("dp"), lax.axis_index("tensor")


def spread_offsets():
    sets = []
    for offset in ((x, y, z) for x in range(SIDE) for y in range(SIDE) for z in range(SIDE)):
        turns = [offset[turn:] + offset[:turn] for turn in range(3)]
        alike = dict.fromkeys(tuple(sign * step % SIDE for step in turn) for sign in (1, -1) for turn in turns)
        if offset == min(alike):
            sets.append(list(alike))
    hops = [sum(min(step, SIDE - step) for step in alike[0]) for alike in sets]
    ranked, rest = [], {}
    for index in range(1, len(sets)):
        rest.setdefault(hops[index], []).append(index)
    while any(rest.values()):
        for some in rest.values():
            if some:
                ranked.append(some.pop())
    return [offset for index in [0, *ranked] for offset in sets[index]]


OFFSETS = spread_offsets()


def targets(sign):
    place, core = position()
    sign = sign * (1 - 2 * core)
    steps = []
    for scale in (SIDE * SIDE, SIDE, 1):
        here = place // scale % SIDE
        steps.append([(here + sign * away + SIDE) % SIDE * scale for away in range(SIDE)])
    return [steps[0][x] + steps[1][y] + steps[2][z] for x, y, z in OFFSETS]


def line_of(row, tile):
    return tile * LOCAL + row


def write_lines(scratch, row, tile, values):
    scratch[pl.ds(line_of(row, tile), 8, stride=PITCH), :] = values


def read_lines(scratch, row, tile):
    return scratch[pl.ds(line_of(row, tile), 8, stride=PITCH), :]


def pack_eight(scratch, blocks, first):
    for item in range(8):
        for part in range(LINES // 8):
            values = scratch[pl.ds(item * PITCH + 8 * part, 8), :]
            blocks[first + item, :, part * LANES : (part + 1) * LANES] = values.astype(jnp.bfloat16)


def unpack_eight(scratch, blocks, first):
    for item in range(8):
        values = blocks[first + item].astype(jnp.float32)
        for part in range(LINES // 8):
            scratch[pl.ds(item * PITCH + 8 * part, 8), :] = values[:, part * LANES : (part + 1) * LANES]


def product(a, b, dims):
    return lax.dot_general(a, b, (dims, ((), ())), preferred_element_type=jnp.float32)


def strip(index):
    return slice(index * TILE, (index + 1) * TILE)


def gram_block(x_ref, i, j):
    return product(x_ref[strip(i), :], x_ref[strip(j), :], ((1,), (1,)))


def keep_block(gram, low, i, j, value):
    gram[strip(i), strip(j)] = value
    low[strip(i), strip(j)] = value.astype(jnp.bfloat16)
    if i != j:
        low[strip(j), strip(i)] = value.T.astype(jnp.bfloat16)


def lay_out(lines, blocks, group, write, sums=None):
    for eight in range(2):
        unpack_eight(lines.at[eight], blocks, group * GROUP + eight * 8)
    for row in range(LOCAL):
        for tile in range(TILES):
            values = [read_lines(lines.at[eight], row, tile) for eight in range(2)]
            write(row, tile, jnp.concatenate(values, axis=0).astype(jnp.bfloat16))
            for index, value in enumerate(values if sums else ()):
                sums[2 * (tile % 2) + index] += value * value


def share_rows(group, core=0):
    return (2 * group + core) * LOCAL * GROUP


def mixer_of(gram, low, mixer, j):
    column = slice(j * TILE, ROWS)
    square = product(low[column, :], low[:, strip(j)], ((1,), (0,)))
    value = cubic_term * gram[column, strip(j)] + quintic_term * square
    mixer[column, strip(j)] = value.astype(jnp.bfloat16)
    for i in range(j + 1, STRIPS):
        mixer[strip(j), strip(i)] = value[strip(i - j), :].T.astype(jnp.bfloat16)


def kernel(
    momentum, gradient, assignment, momentum_new, returned,
    mom_in, grad_in, sent, arrived, relayed, x_now, x_next, gram, low, mixer, lines, squares,
    load_sems, out_sem, in_sems, back_out_sem, back_sem, pair_out_sem, pair_sems,
):
    place, core = position()
    pair = (place, 1 - core)

    def load(group):
        rows = pl.ds(pl.multiple_of(group * GROUP, GROUP), GROUP)
        return (
            pltpu.make_async_copy(momentum.at[:, rows, :], mom_in.at[group], load_sems.at[0, group]),
            pltpu.make_async_copy(gradient.at[:, rows, :], grad_in.at[group], load_sems.at[1, group]),
        )

    for group in range(GROUPS):
        for copy in load(group):
            copy.start()

    barrier = pltpu.get_barrier_semaphore()
    pl.semaphore_signal(barrier, inc=1, device_id=pair, device_id_type=MESH)

    ahead = targets(1)
    for target in ahead[1:]:
        pl.semaphore_signal(barrier, inc=1, device_id=(target, core), device_id_type=MESH)

    def prepare(group, carry):
        for copy in load(group):
            copy.wait()
        rows = pl.ds(pl.multiple_of(group * GROUP, GROUP), GROUP)
        for row in range(LOCAL):
            for tile in range(TILES):
                columns = slice(tile * LANES, (tile + 1) * LANES)
                wide = grad_in[group, row, :, columns].astype(jnp.float32)
                fresh = momentum_rate * mom_in[group, row, :, columns] + wide
                momentum_new[row, rows, columns] = fresh
                direction = wide + momentum_rate * fresh
                for eight in range(2):
                    write_lines(lines.at[eight], row, tile, direction[eight * 8 : eight * 8 + 8])
        for eight in range(2):
            pack_eight(lines.at[eight], sent, group * GROUP + eight * 8)
        return carry

    lax.fori_loop(0, GROUPS, prepare, 0)

    pl.semaphore_wait(barrier, CHIPS)

    pltpu.make_async_copy(sent.at[place], arrived.at[0], in_sems.at[0]).start()

    for slot, target in enumerate(ahead):
        if slot:
            pltpu.make_async_remote_copy(
                src_ref=sent.at[target], dst_ref=arrived.at[slot], send_sem=out_sem, recv_sem=in_sems.at[slot // PIECE],
                device_id=(target, core), device_id_type=MESH,
            ).start()

    def accept(blocks, group, which):
        def write(row, tile, values):
            start = share_rows(group, which) + row * GROUP
            x_now[start : start + GROUP, tile * LANES : (tile + 1) * LANES] = values

        sums = [jnp.zeros((8, LANES), jnp.float32)] * 4
        lay_out(lines, blocks, group, write, sums)
        squares[...] += (sums[0] + sums[1]) + (sums[2] + sums[3])

    def accept_pair(group):
        span = relayed.at[pl.ds(group * GROUP, GROUP)]
        pltpu.make_async_copy(span, span, pair_sems.at[group]).wait()
        accept(relayed, group, 1)
        for i in range(STRIPS - 1):
            if share_rows(group) < (i + 1) * TILE <= share_rows(group + 1):
                for j in range(i + 1):
                    gram[strip(i), strip(j)] = gram_block(x_now, i, j)

    squares[...] = jnp.zeros_like(squares)
    for group in range(GROUPS):
        if group:
            accept_pair(group - 1)
        for piece in range(group * GROUP // PIECE, (group + 1) * GROUP // PIECE):
            span = pl.ds(piece * PIECE, PIECE)
            pltpu.make_async_copy(arrived.at[span], arrived.at[span], in_sems.at[piece]).wait()
            pltpu.make_async_remote_copy(
                src_ref=arrived.at[span], dst_ref=relayed.at[span], send_sem=pair_out_sem, recv_sem=pair_sems.at[group],
                device_id=pair, device_id_type=MESH,
            ).start()
        accept(arrived, group, 0)
    accept_pair(GROUPS - 1)

    scale = 1.0 / (jnp.sqrt(jnp.sum(squares[...])) + epsilon_norm)

    def scaled(value):
        return jnp.where(scale > 0.0, value * scale * scale, 0.0)

    before = [(i, j) for i in range(STRIPS - 1) for j in range(i + 1)]
    for j in range(STRIPS):
        keep_block(gram, low, STRIPS - 1, j, scaled(gram_block(x_now, STRIPS - 1, j)))
        for i, k in before[j::STRIPS]:
            keep_block(gram, low, i, k, scaled(gram[strip(i), strip(k)]))

    for j in range(STRIPS):
        mixer_of(gram, low, mixer, j)

    for index in range(WIDTH // TILE):
        start = (x_now[:, strip(index)].astype(jnp.float32) * scale).astype(jnp.bfloat16)
        value = product(mixer[...], start, ((1,), (0,)))
        x_next[:, strip(index)] = (linear_term * start.astype(jnp.float32) + value).astype(jnp.bfloat16)

    for i in range(STRIPS):
        for j in range(i + 1):
            keep_block(gram, low, i, j, gram_block(x_next, i, j))

    active = assignment[place] >= 0
    made = set()

    def finish(first, last):
        for group in range(first, last):
            for j in range(STRIPS):
                if j not in made and share_rows(group) < (j + 1) * TILE and j * TILE < share_rows(group, 1):
                    made.add(j)
                    mixer_of(gram, low, mixer, j)
        rows = [slice(share_rows(group), share_rows(group, 1)) for group in range(first, last)]

        def gathered(ref):
            parts = [ref[row, :] for row in rows]
            return parts[0] if len(parts) == 1 else jnp.concatenate(parts, axis=0)

        value = linear_term * gathered(x_next).astype(jnp.float32) + product(
            gathered(mixer), x_next[...], ((1,), (0,))
        )
        value = math.sqrt(WIDTH) * value.astype(jnp.bfloat16).astype(jnp.float32)
        value = jnp.where(active, value, 0.0)
        for group in range(first, last):
            for eight in range(2):
                place_lines = lines.at[2 * (group - first) + eight]
                for row in range(LOCAL):
                    start = (group - first) * LOCAL * GROUP + row * GROUP + eight * 8
                    for tile in range(TILES):
                        write_lines(
                            place_lines, row, tile, value[start : start + 8, tile * LANES : (tile + 1) * LANES]
                        )
                pack_eight(place_lines, sent, group * GROUP + eight * 8)

    gone = sent.at[pl.ds(1, CHIPS - 1)]
    pltpu.make_async_copy(gone, gone, out_sem).wait()
    behind = targets(-1)
    for first, last in SHARES:
        finish(first, last)
        for slot in range(first * GROUP, last * GROUP):
            if slot == 0:
                pltpu.make_async_copy(sent.at[0], returned.at[place], back_sem).start()
            else:
                pltpu.make_async_remote_copy(
                    src_ref=sent.at[slot], dst_ref=returned.at[place], send_sem=back_out_sem, recv_sem=back_sem,
                    device_id=(behind[slot], core), device_id_type=MESH,
                ).start()

    pltpu.make_async_copy(arrived, arrived, pair_out_sem).wait()
    pltpu.make_async_copy(returned, returned, back_sem).wait()
    pltpu.make_async_copy(gone, gone, back_out_sem).wait()


def place_results(fresh, returned, momentum_new, update, rows_out, lines, fresh_sem, group_sems):
    whole = pltpu.make_async_copy(fresh, momentum_new, fresh_sem)
    whole.start()
    copies = []
    for group in range(GROUPS):
        rows = pl.ds(group * GROUP, GROUP)

        def write(row, tile, values):
            rows_out[row, group * GROUP : (group + 1) * GROUP, tile * LANES : (tile + 1) * LANES] = values

        lay_out(lines, returned, group, write)
        copies.append(
            pltpu.make_async_copy(rows_out.at[:, rows, :], update.at[:, rows, :], group_sems.at[group])
        )
        copies[-1].start()
    for copy in copies:
        copy.wait()
    whole.wait()


def on_device(momentum, gradient, assignment):
    shape = (LOCAL, CHIPS, WIDTH)
    blocks = pltpu.VMEM((CHIPS, *BLOCK), jnp.bfloat16)
    line_space = pltpu.VMEM((2 * GROUPS, 8 * PITCH, LANES), jnp.float32)
    fresh, returned = pl.pallas_call(
        kernel,
        out_shape=(pltpu.VMEM(shape, jnp.float32), blocks),
        in_specs=[
            pl.BlockSpec(memory_space=pl.ANY),
            pl.BlockSpec(memory_space=pl.ANY),
            pl.BlockSpec(memory_space=pltpu.SMEM),
        ],
        out_specs=[pl.BlockSpec(memory_space=pltpu.VMEM)] * 2,
        scratch_shapes=[
            pltpu.VMEM((GROUPS, LOCAL, GROUP, WIDTH), jnp.float32),
            pltpu.VMEM((GROUPS, LOCAL, GROUP, WIDTH), jnp.bfloat16),
            blocks,
            blocks,
            blocks,
            pltpu.VMEM((ROWS, WIDTH), jnp.bfloat16),
            pltpu.VMEM((ROWS, WIDTH), jnp.bfloat16),
            pltpu.VMEM((ROWS, ROWS), jnp.float32),
            pltpu.VMEM((ROWS, ROWS), jnp.bfloat16),
            pltpu.VMEM((ROWS, ROWS), jnp.bfloat16),
            line_space,
            pltpu.VMEM((8, LANES), jnp.float32),
            pltpu.SemaphoreType.DMA((2, GROUPS)),
            pltpu.SemaphoreType.DMA,
            pltpu.SemaphoreType.DMA((PIECES,)),
            pltpu.SemaphoreType.DMA,
            pltpu.SemaphoreType.DMA,
            pltpu.SemaphoreType.DMA,
            pltpu.SemaphoreType.DMA((GROUPS,)),
        ],
        compiler_params=pltpu.CompilerParams(
            collective_id=0, has_side_effects=True, vmem_limit_bytes=50 * 2**20
        ),
        name="muon",
    )(jnp.transpose(momentum, (1, 0, 2)), jnp.transpose(gradient, (1, 0, 2)), assignment)
    momentum_new, update = pl.pallas_call(
        place_results,
        out_shape=(jax.ShapeDtypeStruct(shape, jnp.float32), jax.ShapeDtypeStruct(shape, jnp.bfloat16)),
        in_specs=[pl.BlockSpec(memory_space=pltpu.VMEM)] * 2,
        out_specs=[pl.BlockSpec(memory_space=pl.ANY)] * 2,
        scratch_shapes=[
            pltpu.VMEM(shape, jnp.bfloat16),
            line_space,
            pltpu.SemaphoreType.DMA,
            pltpu.SemaphoreType.DMA((GROUPS,)),
        ],
        compiler_params=pltpu.CompilerParams(vmem_limit_bytes=32 * 2**20),
        name="place_results",
    )(fresh, returned)
    return jnp.transpose(momentum_new, (1, 0, 2)), jnp.transpose(update, (1, 0, 2))


def solution(mesh):
    placed = P(None, ("dp", "tensor"), None)
    return jax.shard_map(
        on_device,
        mesh=mesh,
        in_specs=(placed, placed, P()),
        out_specs=(placed, placed),
        check_vma=False,
    )
```

```python
import math

import jax
import jax.numpy as jnp
from jax import lax
from jax.experimental import pallas as pl
from jax.experimental.pallas import tpu as pltpu
from jax.sharding import PartitionSpec as P

ITERS = 2
MESH = pl.DeviceIdType.MESH

momentum_rate = 0.95
epsilon_norm = 1e-07
linear_term = 3.4445
cubic_term = -4.775
quintic_term = 2.0315

SIDE = 4
CHIPS = SIDE**3
LOCAL = 6
WIDTH = 2560
LANES = 128
TILES = WIDTH // LANES
ROWS = LOCAL * CHIPS * 2
HALF = LOCAL * CHIPS
LINES = LOCAL * TILES
BLOCK = (8, LINES // 8 * LANES)
PITCH = LINES + 1
GROUP = 16
GROUPS = CHIPS // GROUP
PIECE = 4
PIECES = CHIPS // PIECE
SHARES = ((0, 1), (1, GROUPS))
TILE = 256
STRIPS = ROWS // TILE


def position():
    return lax.axis_index("dp"), lax.axis_index("tensor")


def spread_offsets():
    sets = []
    for offset in ((x, y, z) for x in range(SIDE) for y in range(SIDE) for z in range(SIDE)):
        turns = [offset[turn:] + offset[:turn] for turn in range(3)]
        alike = dict.fromkeys(tuple(sign * step % SIDE for step in turn) for sign in (1, -1) for turn in turns)
        if offset == min(alike):
            sets.append(list(alike))
    hops = [sum(min(step, SIDE - step) for step in alike[0]) for alike in sets]
    ranked, rest = [], {}
    for index in range(1, len(sets)):
        rest.setdefault(hops[index], []).append(index)
    while any(rest.values()):
        for some in rest.values():
            if some:
                ranked.append(some.pop())
    return [offset for index in [0, *ranked] for offset in sets[index]]


OFFSETS = spread_offsets()


def targets(sign):
    place, _ = position()
    steps = []
    for scale in (SIDE * SIDE, SIDE, 1):
        here = place // scale % SIDE
        steps.append([(here + sign * away + SIDE) % SIDE * scale for away in range(SIDE)])
    return [steps[0][x] + steps[1][y] + steps[2][z] for x, y, z in OFFSETS]


def line_of(row, tile):
    return tile * LOCAL + row


def write_lines(scratch, row, tile, values):
    scratch[pl.ds(line_of(row, tile), 8, stride=PITCH), :] = values


def read_lines(scratch, row, tile):
    return scratch[pl.ds(line_of(row, tile), 8, stride=PITCH), :]


def pack_eight(scratch, blocks, first):
    for item in range(8):
        for part in range(LINES // 8):
            values = scratch[pl.ds(item * PITCH + 8 * part, 8), :]
            blocks[first + item, :, part * LANES : (part + 1) * LANES] = values.astype(jnp.bfloat16)


def unpack_eight(scratch, blocks, first):
    for item in range(8):
        values = blocks[first + item].astype(jnp.float32)
        for part in range(LINES // 8):
            scratch[pl.ds(item * PITCH + 8 * part, 8), :] = values[:, part * LANES : (part + 1) * LANES]


def product(a, b, dims):
    return lax.dot_general(a, b, (dims, ((), ())), preferred_element_type=jnp.float32)


def strip(index):
    return slice(index * TILE, (index + 1) * TILE)


def gram_block(x_ref, i, j):
    return product(x_ref[strip(i), :], x_ref[strip(j), :], ((1,), (1,)))


def keep_block(gram, low, i, j, value):
    gram[strip(i), strip(j)] = value
    low[strip(i), strip(j)] = value.astype(jnp.bfloat16)
    if i != j:
        low[strip(j), strip(i)] = value.T.astype(jnp.bfloat16)


def lay_out(lines, blocks, group, write, sums=None):
    for eight in range(2):
        unpack_eight(lines.at[eight], blocks, group * GROUP + eight * 8)
    for row in range(LOCAL):
        for tile in range(TILES):
            values = [read_lines(lines.at[eight], row, tile) for eight in range(2)]
            write(row, tile, jnp.concatenate(values, axis=0).astype(jnp.bfloat16))
            for index, value in enumerate(values if sums else ()):
                sums[2 * (tile % 2) + index] += value * value


def share_rows(group, core=0):
    return (2 * group + core) * LOCAL * GROUP


def mixer_of(gram, low, mixer, j):
    column = slice(j * TILE, ROWS)
    square = product(low[column, :], low[:, strip(j)], ((1,), (0,)))
    value = cubic_term * gram[column, strip(j)] + quintic_term * square
    mixer[column, strip(j)] = value.astype(jnp.bfloat16)
    for i in range(j + 1, STRIPS):
        mixer[strip(j), strip(i)] = value[strip(i - j), :].T.astype(jnp.bfloat16)


def kernel(
    momentum, gradient, assignment, momentum_new, returned,
    mom_in, grad_in, sent, arrived, relayed, x_now, x_next, gram, low, mixer, lines, squares, owners,
    plane_sem, owner_sem, load_sems, out_sem, in_sems, back_out_sem, back_sem, pair_out_sem, pair_sems,
):
    place, core = position()
    pair = (place, 1 - core)

    def load(group):
        rows = pl.ds(pl.multiple_of(group * GROUP, GROUP), GROUP)
        return (
            pltpu.make_async_copy(momentum.at[:, rows, :], mom_in.at[group], load_sems.at[0, group]),
            pltpu.make_async_copy(gradient.at[:, rows, :], grad_in.at[group], load_sems.at[1, group]),
        )

    for group in range(GROUPS):
        for copy in load(group):
            copy.start()
    fetch = pltpu.make_async_copy(assignment, owners, owner_sem)
    fetch.start()

    barrier = pltpu.get_barrier_semaphore()
    pl.semaphore_signal(barrier, inc=1, device_id=pair, device_id_type=MESH)

    ahead = targets(1)
    plane = [target for target, offset in zip(ahead, OFFSETS) if offset[2] == 0][1:]
    line = [target for target, offset in zip(ahead, OFFSETS) if offset[:2] == (0, 0)][1:]
    for target in plane + line:
        pl.semaphore_signal(barrier, inc=1, device_id=(target, core), device_id_type=MESH)

    def prepare(group, carry):
        for copy in load(group):
            copy.wait()
        rows = pl.ds(pl.multiple_of(group * GROUP, GROUP), GROUP)
        for row in range(LOCAL):
            for tile in range(TILES):
                columns = slice(tile * LANES, (tile + 1) * LANES)
                wide = grad_in[group, row, :, columns].astype(jnp.float32)
                fresh = momentum_rate * mom_in[group, row, :, columns] + wide
                momentum_new[row, rows, columns] = fresh
                direction = wide + momentum_rate * fresh
                for eight in range(2):
                    write_lines(lines.at[eight], row, tile, direction[eight * 8 : eight * 8 + 8])
        for eight in range(2):
            pack_eight(lines.at[eight], sent, group * GROUP + eight * 8)
        return carry

    lax.fori_loop(0, GROUPS // 2, prepare, 0)
    pl.semaphore_wait(barrier, 1 + len(plane) + len(line))
    for target in line:
        pl.semaphore_signal(plane_sem, inc=1, device_id=(target, core), device_id_type=MESH)
    lax.fori_loop(GROUPS // 2, GROUPS, prepare, 0)
    pl.semaphore_wait(plane_sem, len(line))

    pltpu.make_async_copy(sent.at[place], arrived.at[0], in_sems.at[0]).start()

    for slot, target in enumerate(ahead):
        if slot:
            pltpu.make_async_remote_copy(
                src_ref=sent.at[target], dst_ref=arrived.at[slot], send_sem=out_sem, recv_sem=in_sems.at[slot // PIECE],
                device_id=(target, core), device_id_type=MESH,
            ).start()

    def accept(blocks, group, which):
        def write(row, tile, values):
            start = share_rows(group, which) + row * GROUP
            x_now[start : start + GROUP, tile * LANES : (tile + 1) * LANES] = values

        sums = [jnp.zeros((8, LANES), jnp.float32)] * 4
        lay_out(lines, blocks, group, write, sums)
        squares[...] += (sums[0] + sums[1]) + (sums[2] + sums[3])

    def accept_pair(group):
        span = relayed.at[pl.ds(group * GROUP, GROUP)]
        pltpu.make_async_copy(span, span, pair_sems.at[group]).wait()
        accept(relayed, group, 1)
        for i in range(STRIPS - 1):
            if share_rows(group) < (i + 1) * TILE <= share_rows(group + 1):
                for j in range(i + 1):
                    gram[strip(i), strip(j)] = gram_block(x_now, i, j)

    squares[...] = jnp.zeros_like(squares)
    for group in range(GROUPS):
        if group:
            accept_pair(group - 1)
        for piece in range(group * GROUP // PIECE, (group + 1) * GROUP // PIECE):
            span = pl.ds(piece * PIECE, PIECE)
            pltpu.make_async_copy(arrived.at[span], arrived.at[span], in_sems.at[piece]).wait()
            pltpu.make_async_remote_copy(
                src_ref=arrived.at[span], dst_ref=relayed.at[span], send_sem=pair_out_sem, recv_sem=pair_sems.at[group],
                device_id=pair, device_id_type=MESH,
            ).start()
        accept(arrived, group, 0)
    accept_pair(GROUPS - 1)

    scale = 1.0 / (jnp.sqrt(jnp.sum(squares[...])) + epsilon_norm)

    def scaled(value):
        return jnp.where(scale > 0.0, value * scale * scale, 0.0)

    before = [(i, j) for i in range(STRIPS - 1) for j in range(i + 1)]
    for j in range(STRIPS):
        keep_block(gram, low, STRIPS - 1, j, scaled(gram_block(x_now, STRIPS - 1, j)))
        for i, k in before[j::STRIPS]:
            keep_block(gram, low, i, k, scaled(gram[strip(i), strip(k)]))

    for j in range(STRIPS):
        mixer_of(gram, low, mixer, j)

    for index in range(WIDTH // TILE):
        start = (x_now[:, strip(index)].astype(jnp.float32) * scale).astype(jnp.bfloat16)
        value = product(mixer[...], start, ((1,), (0,)))
        x_next[:, strip(index)] = (linear_term * start.astype(jnp.float32) + value).astype(jnp.bfloat16)

    for i in range(STRIPS):
        for j in range(i + 1):
            keep_block(gram, low, i, j, gram_block(x_next, i, j))

    fetch.wait()
    active = owners[place] >= 0
    made = set()

    def finish(first, last):
        for group in range(first, last):
            for j in range(STRIPS):
                if j not in made and share_rows(group) < (j + 1) * TILE and j * TILE < share_rows(group, 1):
                    made.add(j)
                    mixer_of(gram, low, mixer, j)
        rows = [slice(share_rows(group), share_rows(group, 1)) for group in range(first, last)]

        def gathered(ref):
            parts = [ref[row, :] for row in rows]
            return parts[0] if len(parts) == 1 else jnp.concatenate(parts, axis=0)

        value = linear_term * gathered(x_next).astype(jnp.float32) + product(
            gathered(mixer), x_next[...], ((1,), (0,))
        )
        value = math.sqrt(WIDTH) * value.astype(jnp.bfloat16).astype(jnp.float32)
        value = jnp.where(active, value, 0.0)
        for group in range(first, last):
            for eight in range(2):
                place_lines = lines.at[2 * (group - first) + eight]
                for row in range(LOCAL):
                    start = (group - first) * LOCAL * GROUP + row * GROUP + eight * 8
                    for tile in range(TILES):
                        write_lines(
                            place_lines, row, tile, value[start : start + 8, tile * LANES : (tile + 1) * LANES]
                        )
                pack_eight(place_lines, sent, group * GROUP + eight * 8)

    gone = sent.at[pl.ds(1, CHIPS - 1)]
    pltpu.make_async_copy(gone, gone, out_sem).wait()
    behind = targets(-1)
    for first, last in SHARES:
        finish(first, last)
        for slot in range(first * GROUP, last * GROUP):
            if slot == 0:
                pltpu.make_async_copy(sent.at[0], returned.at[place], back_sem).start()
            else:
                pltpu.make_async_remote_copy(
                    src_ref=sent.at[slot], dst_ref=returned.at[place], send_sem=back_out_sem, recv_sem=back_sem,
                    device_id=(behind[slot], core), device_id_type=MESH,
                ).start()

    pltpu.make_async_copy(arrived, arrived, pair_out_sem).wait()
    pltpu.make_async_copy(returned, returned, back_sem).wait()
    pltpu.make_async_copy(gone, gone, back_out_sem).wait()


def place_results(fresh, returned, momentum_new, update, rows_out, lines, fresh_sem, group_sems):
    whole = pltpu.make_async_copy(fresh, momentum_new, fresh_sem)
    whole.start()
    copies = []
    for group in range(GROUPS):
        rows = pl.ds(group * GROUP, GROUP)

        def write(row, tile, values):
            rows_out[row, group * GROUP : (group + 1) * GROUP, tile * LANES : (tile + 1) * LANES] = values

        lay_out(lines, returned, group, write)
        copies.append(
            pltpu.make_async_copy(rows_out.at[:, rows, :], update.at[:, rows, :], group_sems.at[group])
        )
        copies[-1].start()
    for copy in copies:
        copy.wait()
    whole.wait()


def on_device(momentum, gradient, assignment):
    shape = (LOCAL, CHIPS, WIDTH)
    blocks = pltpu.VMEM((CHIPS, *BLOCK), jnp.bfloat16)
    line_space = pltpu.VMEM((2 * GROUPS, 8 * PITCH, LANES), jnp.float32)
    fresh, returned = pl.pallas_call(
        kernel,
        out_shape=(pltpu.VMEM(shape, jnp.float32), blocks),
        in_specs=[
            pl.BlockSpec(memory_space=pl.ANY),
            pl.BlockSpec(memory_space=pl.ANY),
            pl.BlockSpec(memory_space=pl.ANY),
        ],
        out_specs=[pl.BlockSpec(memory_space=pltpu.VMEM)] * 2,
        scratch_shapes=[
            pltpu.VMEM((GROUPS, LOCAL, GROUP, WIDTH), jnp.float32),
            pltpu.VMEM((GROUPS, LOCAL, GROUP, WIDTH), jnp.bfloat16),
            blocks,
            blocks,
            blocks,
            pltpu.VMEM((ROWS, WIDTH), jnp.bfloat16),
            pltpu.VMEM((ROWS, WIDTH), jnp.bfloat16),
            pltpu.VMEM((ROWS, ROWS), jnp.float32),
            pltpu.VMEM((ROWS, ROWS), jnp.bfloat16),
            pltpu.VMEM((ROWS, ROWS), jnp.bfloat16),
            line_space,
            pltpu.VMEM((8, LANES), jnp.float32),
            pltpu.SMEM((CHIPS,), jnp.int32),
            pltpu.SemaphoreType.REGULAR,
            pltpu.SemaphoreType.DMA,
            pltpu.SemaphoreType.DMA((2, GROUPS)),
            pltpu.SemaphoreType.DMA,
            pltpu.SemaphoreType.DMA((PIECES,)),
            pltpu.SemaphoreType.DMA,
            pltpu.SemaphoreType.DMA,
            pltpu.SemaphoreType.DMA,
            pltpu.SemaphoreType.DMA((GROUPS,)),
        ],
        compiler_params=pltpu.CompilerParams(
            collective_id=0, has_side_effects=True, vmem_limit_bytes=50 * 2**20
        ),
        name="muon",
    )(jnp.transpose(momentum, (1, 0, 2)), jnp.transpose(gradient, (1, 0, 2)), assignment)
    momentum_new, update = pl.pallas_call(
        place_results,
        out_shape=(jax.ShapeDtypeStruct(shape, jnp.float32), jax.ShapeDtypeStruct(shape, jnp.bfloat16)),
        in_specs=[pl.BlockSpec(memory_space=pltpu.VMEM)] * 2,
        out_specs=[pl.BlockSpec(memory_space=pl.ANY)] * 2,
        scratch_shapes=[
            pltpu.VMEM(shape, jnp.bfloat16),
            line_space,
            pltpu.SemaphoreType.DMA,
            pltpu.SemaphoreType.DMA((GROUPS,)),
        ],
        compiler_params=pltpu.CompilerParams(vmem_limit_bytes=32 * 2**20),
        name="place_results",
    )(fresh, returned)
    return jnp.transpose(momentum_new, (1, 0, 2)), jnp.transpose(update, (1, 0, 2))


def solution(mesh):
    placed = P(None, ("dp", "tensor"), None)
    return jax.shard_map(
        on_device,
        mesh=mesh,
        in_specs=(placed, placed, P()),
        out_specs=(placed, placed),
        check_vma=False,
    )
```

```python
import math

import jax
import jax.numpy as jnp
from jax import lax
from jax.experimental import pallas as pl
from jax.experimental.pallas import tpu as pltpu
from jax.sharding import PartitionSpec as P

ITERS = 2
MESH = pl.DeviceIdType.MESH

momentum_rate = 0.95
epsilon_norm = 1e-07
linear_term = 3.4445
cubic_term = -4.775
quintic_term = 2.0315

SIDE = 4
CHIPS = SIDE**3
LOCAL = 6
WIDTH = 2560
LANES = 128
TILES = WIDTH // LANES
ROWS = LOCAL * CHIPS * 2
HALF = LOCAL * CHIPS
LINES = LOCAL * TILES
BLOCK = (8, LINES // 8 * LANES)
PITCH = LINES + 1
GROUP = 16
GROUPS = CHIPS // GROUP
PIECE = 4
PIECES = CHIPS // PIECE
SHARES = tuple((group, group + 1) for group in range(GROUPS))
TILE = 256
STRIPS = ROWS // TILE


def position():
    return lax.axis_index("dp"), lax.axis_index("tensor")


def spread_offsets():
    sets = []
    for offset in ((x, y, z) for x in range(SIDE) for y in range(SIDE) for z in range(SIDE)):
        turns = [offset[turn:] + offset[:turn] for turn in range(3)]
        alike = dict.fromkeys(tuple(sign * step % SIDE for step in turn) for sign in (1, -1) for turn in turns)
        if offset == min(alike):
            sets.append(list(alike))
    hops = [sum(min(step, SIDE - step) for step in alike[0]) for alike in sets]
    ranked, rest = [], {}
    for index in range(1, len(sets)):
        rest.setdefault(hops[index], []).append(index)
    while any(rest.values()):
        for some in rest.values():
            if some:
                ranked.append(some.pop())
    return [offset for index in [0, *ranked] for offset in sets[index]]


OFFSETS = spread_offsets()


def targets(sign):
    place, _ = position()
    steps = []
    for scale in (SIDE * SIDE, SIDE, 1):
        here = place // scale % SIDE
        steps.append([(here + sign * away + SIDE) % SIDE * scale for away in range(SIDE)])
    return [steps[0][x] + steps[1][y] + steps[2][z] for x, y, z in OFFSETS]


def line_of(row, tile):
    return tile * LOCAL + row


def write_lines(scratch, row, tile, values):
    scratch[pl.ds(line_of(row, tile), 8, stride=PITCH), :] = values


def read_lines(scratch, row, tile):
    return scratch[pl.ds(line_of(row, tile), 8, stride=PITCH), :]


def pack_eight(scratch, blocks, first):
    for item in range(8):
        for part in range(LINES // 8):
            values = scratch[pl.ds(item * PITCH + 8 * part, 8), :]
            blocks[first + item, :, part * LANES : (part + 1) * LANES] = values.astype(jnp.bfloat16)


def unpack_eight(scratch, blocks, first):
    for item in range(8):
        values = blocks[first + item].astype(jnp.float32)
        for part in range(LINES // 8):
            scratch[pl.ds(item * PITCH + 8 * part, 8), :] = values[:, part * LANES : (part + 1) * LANES]


def product(a, b, dims):
    return lax.dot_general(a, b, (dims, ((), ())), preferred_element_type=jnp.float32)


def strip(index):
    return slice(index * TILE, (index + 1) * TILE)


def gram_block(x_ref, i, j):
    return product(x_ref[strip(i), :], x_ref[strip(j), :], ((1,), (1,)))


def keep_block(gram, low, i, j, value):
    gram[strip(i), strip(j)] = value
    low[strip(i), strip(j)] = value.astype(jnp.bfloat16)
    if i != j:
        low[strip(j), strip(i)] = value.T.astype(jnp.bfloat16)


def lay_out(lines, blocks, group, write, sums=None):
    for eight in range(2):
        unpack_eight(lines.at[eight], blocks, group * GROUP + eight * 8)
    for row in range(LOCAL):
        for tile in range(TILES):
            values = [read_lines(lines.at[eight], row, tile) for eight in range(2)]
            write(row, tile, jnp.concatenate(values, axis=0).astype(jnp.bfloat16))
            for index, value in enumerate(values if sums else ()):
                sums[2 * (tile % 2) + index] += value * value


def share_rows(group, core=0):
    return (2 * group + core) * LOCAL * GROUP


def mixer_of(gram, low, mixer, j):
    column = slice(j * TILE, ROWS)
    square = product(low[column, :], low[:, strip(j)], ((1,), (0,)))
    value = cubic_term * gram[column, strip(j)] + quintic_term * square
    mixer[column, strip(j)] = value.astype(jnp.bfloat16)
    for i in range(j + 1, STRIPS):
        mixer[strip(j), strip(i)] = value[strip(i - j), :].T.astype(jnp.bfloat16)


def kernel(
    momentum, gradient, assignment, momentum_new, returned,
    mom_in, grad_in, sent, arrived, relayed, x_now, x_next, gram, low, mixer, lines, squares, owners,
    plane_sem, owner_sem, load_sems, out_sem, in_sems, back_out_sem, back_sem, pair_out_sem, pair_sems,
):
    place, core = position()
    pair = (place, 1 - core)

    def load(group):
        rows = pl.ds(pl.multiple_of(group * GROUP, GROUP), GROUP)
        return (
            pltpu.make_async_copy(momentum.at[:, rows, :], mom_in.at[group], load_sems.at[0, group]),
            pltpu.make_async_copy(gradient.at[:, rows, :], grad_in.at[group], load_sems.at[1, group]),
        )

    for group in range(GROUPS):
        for copy in load(group):
            copy.start()
    fetch = pltpu.make_async_copy(assignment, owners, owner_sem)
    fetch.start()

    barrier = pltpu.get_barrier_semaphore()
    pl.semaphore_signal(barrier, inc=1, device_id=pair, device_id_type=MESH)

    ahead = targets(1)
    plane = [target for target, offset in zip(ahead, OFFSETS) if offset[2] == 0][1:]
    line = [target for target, offset in zip(ahead, OFFSETS) if offset[:2] == (0, 0)][1:]
    for target in plane + line:
        pl.semaphore_signal(barrier, inc=1, device_id=(target, core), device_id_type=MESH)

    def prepare(group, carry):
        for copy in load(group):
            copy.wait()
        rows = pl.ds(pl.multiple_of(group * GROUP, GROUP), GROUP)
        for row in range(LOCAL):
            for tile in range(TILES):
                columns = slice(tile * LANES, (tile + 1) * LANES)
                wide = grad_in[group, row, :, columns].astype(jnp.float32)
                fresh = momentum_rate * mom_in[group, row, :, columns] + wide
                momentum_new[row, rows, columns] = fresh
                direction = wide + momentum_rate * fresh
                for eight in range(2):
                    write_lines(lines.at[eight], row, tile, direction[eight * 8 : eight * 8 + 8])
        for eight in range(2):
            pack_eight(lines.at[eight], sent, group * GROUP + eight * 8)
        return carry

    lax.fori_loop(0, GROUPS // 2, prepare, 0)
    pl.semaphore_wait(barrier, 1 + len(plane) + len(line))
    for target in line:
        pl.semaphore_signal(plane_sem, inc=1, device_id=(target, core), device_id_type=MESH)
    lax.fori_loop(GROUPS // 2, GROUPS, prepare, 0)
    pl.semaphore_wait(plane_sem, len(line))

    pltpu.make_async_copy(sent.at[place], arrived.at[0], in_sems.at[0]).start()

    for slot, target in enumerate(ahead):
        if slot:
            pltpu.make_async_remote_copy(
                src_ref=sent.at[target], dst_ref=arrived.at[slot], send_sem=out_sem, recv_sem=in_sems.at[slot // PIECE],
                device_id=(target, core), device_id_type=MESH,
            ).start()

    def accept(blocks, group, which):
        def write(row, tile, values):
            start = share_rows(group, which) + row * GROUP
            x_now[start : start + GROUP, tile * LANES : (tile + 1) * LANES] = values

        sums = [jnp.zeros((8, LANES), jnp.float32)] * 4
        lay_out(lines, blocks, group, write, sums)
        squares[...] += (sums[0] + sums[1]) + (sums[2] + sums[3])

    def accept_pair(group):
        span = relayed.at[pl.ds(group * GROUP, GROUP)]
        pltpu.make_async_copy(span, span, pair_sems.at[group]).wait()
        accept(relayed, group, 1)
        for i in range(STRIPS - 1):
            if share_rows(group) < (i + 1) * TILE <= share_rows(group + 1):
                for j in range(i + 1):
                    gram[strip(i), strip(j)] = gram_block(x_now, i, j)

    squares[...] = jnp.zeros_like(squares)
    for group in range(GROUPS):
        if group:
            accept_pair(group - 1)
        for piece in range(group * GROUP // PIECE, (group + 1) * GROUP // PIECE):
            span = pl.ds(piece * PIECE, PIECE)
            pltpu.make_async_copy(arrived.at[span], arrived.at[span], in_sems.at[piece]).wait()
            pltpu.make_async_remote_copy(
                src_ref=arrived.at[span], dst_ref=relayed.at[span], send_sem=pair_out_sem, recv_sem=pair_sems.at[group],
                device_id=pair, device_id_type=MESH,
            ).start()
        accept(arrived, group, 0)
    accept_pair(GROUPS - 1)

    scale = 1.0 / (jnp.sqrt(jnp.sum(squares[...])) + epsilon_norm)

    def scaled(value):
        return jnp.where(scale > 0.0, value * scale * scale, 0.0)

    before = [(i, j) for i in range(STRIPS - 1) for j in range(i + 1)]
    for j in range(STRIPS):
        keep_block(gram, low, STRIPS - 1, j, scaled(gram_block(x_now, STRIPS - 1, j)))
        for i, k in before[j::STRIPS]:
            keep_block(gram, low, i, k, scaled(gram[strip(i), strip(k)]))

    for j in range(STRIPS):
        mixer_of(gram, low, mixer, j)

    for index in range(WIDTH // TILE):
        start = (x_now[:, strip(index)].astype(jnp.float32) * scale).astype(jnp.bfloat16)
        value = product(mixer[...], start, ((1,), (0,)))
        x_next[:, strip(index)] = (linear_term * start.astype(jnp.float32) + value).astype(jnp.bfloat16)

    for i in range(STRIPS):
        for j in range(i + 1):
            keep_block(gram, low, i, j, gram_block(x_next, i, j))

    fetch.wait()
    active = owners[place] >= 0
    made = set()

    def finish(first, last):
        for group in range(first, last):
            for j in range(STRIPS):
                if j not in made and share_rows(group) < (j + 1) * TILE and j * TILE < share_rows(group, 1):
                    made.add(j)
                    mixer_of(gram, low, mixer, j)
        rows = [slice(share_rows(group), share_rows(group, 1)) for group in range(first, last)]

        def gathered(ref):
            parts = [ref[row, :] for row in rows]
            return parts[0] if len(parts) == 1 else jnp.concatenate(parts, axis=0)

        value = linear_term * gathered(x_next).astype(jnp.float32) + product(
            gathered(mixer), x_next[...], ((1,), (0,))
        )
        value = math.sqrt(WIDTH) * value.astype(jnp.bfloat16).astype(jnp.float32)
        value = jnp.where(active, value, 0.0)
        for group in range(first, last):
            for eight in range(2):
                place_lines = lines.at[2 * (group - first) + eight]
                for row in range(LOCAL):
                    start = (group - first) * LOCAL * GROUP + row * GROUP + eight * 8
                    for tile in range(TILES):
                        write_lines(
                            place_lines, row, tile, value[start : start + 8, tile * LANES : (tile + 1) * LANES]
                        )
                pack_eight(place_lines, sent, group * GROUP + eight * 8)

    gone = sent.at[pl.ds(1, CHIPS - 1)]
    pltpu.make_async_copy(gone, gone, out_sem).wait()
    behind = targets(-1)
    for first, last in SHARES:
        finish(first, last)
        for slot in range(first * GROUP, last * GROUP):
            if slot == 0:
                pltpu.make_async_copy(sent.at[0], returned.at[place], back_sem).start()
            else:
                pltpu.make_async_remote_copy(
                    src_ref=sent.at[slot], dst_ref=returned.at[place], send_sem=back_out_sem, recv_sem=back_sem,
                    device_id=(behind[slot], core), device_id_type=MESH,
                ).start()

    pltpu.make_async_copy(arrived, arrived, pair_out_sem).wait()
    pltpu.make_async_copy(returned, returned, back_sem).wait()
    pltpu.make_async_copy(gone, gone, back_out_sem).wait()


def place_results(fresh, returned, momentum_new, update, rows_out, lines, fresh_sem, group_sems):
    copies = [
        pltpu.make_async_copy(fresh.at[row], momentum_new.at[row], fresh_sem.at[row]) for row in range(LOCAL)
    ]
    for copy in copies:
        copy.start()
    for group in range(GROUPS):
        rows = pl.ds(group * GROUP, GROUP)

        def write(row, tile, values):
            rows_out[row, group * GROUP : (group + 1) * GROUP, tile * LANES : (tile + 1) * LANES] = values

        lay_out(lines, returned, group, write)
        copies.append(
            pltpu.make_async_copy(rows_out.at[:, rows, :], update.at[:, rows, :], group_sems.at[group])
        )
        copies[-1].start()
    for copy in copies:
        copy.wait()


def on_device(momentum, gradient, assignment):
    shape = (LOCAL, CHIPS, WIDTH)
    blocks = pltpu.VMEM((CHIPS, *BLOCK), jnp.bfloat16)
    line_space = pltpu.VMEM((2 * GROUPS, 8 * PITCH, LANES), jnp.float32)
    fresh, returned = pl.pallas_call(
        kernel,
        out_shape=(pltpu.VMEM(shape, jnp.float32), blocks),
        in_specs=[
            pl.BlockSpec(memory_space=pl.ANY),
            pl.BlockSpec(memory_space=pl.ANY),
            pl.BlockSpec(memory_space=pl.ANY),
        ],
        out_specs=[pl.BlockSpec(memory_space=pltpu.VMEM)] * 2,
        scratch_shapes=[
            pltpu.VMEM((GROUPS, LOCAL, GROUP, WIDTH), jnp.float32),
            pltpu.VMEM((GROUPS, LOCAL, GROUP, WIDTH), jnp.bfloat16),
            blocks,
            blocks,
            blocks,
            pltpu.VMEM((ROWS, WIDTH), jnp.bfloat16),
            pltpu.VMEM((ROWS, WIDTH), jnp.bfloat16),
            pltpu.VMEM((ROWS, ROWS), jnp.float32),
            pltpu.VMEM((ROWS, ROWS), jnp.bfloat16),
            pltpu.VMEM((ROWS, ROWS), jnp.bfloat16),
            line_space,
            pltpu.VMEM((8, LANES), jnp.float32),
            pltpu.SMEM((CHIPS,), jnp.int32),
            pltpu.SemaphoreType.REGULAR,
            pltpu.SemaphoreType.DMA,
            pltpu.SemaphoreType.DMA((2, GROUPS)),
            pltpu.SemaphoreType.DMA,
            pltpu.SemaphoreType.DMA((PIECES,)),
            pltpu.SemaphoreType.DMA,
            pltpu.SemaphoreType.DMA,
            pltpu.SemaphoreType.DMA,
            pltpu.SemaphoreType.DMA((GROUPS,)),
        ],
        compiler_params=pltpu.CompilerParams(
            collective_id=0, has_side_effects=True, vmem_limit_bytes=50 * 2**20
        ),
        name="muon",
    )(jnp.transpose(momentum, (1, 0, 2)), jnp.transpose(gradient, (1, 0, 2)), assignment)
    momentum_new, update = pl.pallas_call(
        place_results,
        out_shape=(jax.ShapeDtypeStruct(shape, jnp.float32), jax.ShapeDtypeStruct(shape, jnp.bfloat16)),
        in_specs=[pl.BlockSpec(memory_space=pltpu.VMEM)] * 2,
        out_specs=[pl.BlockSpec(memory_space=pl.ANY)] * 2,
        scratch_shapes=[
            pltpu.VMEM(shape, jnp.bfloat16),
            line_space,
            pltpu.SemaphoreType.DMA((LOCAL,)),
            pltpu.SemaphoreType.DMA((GROUPS,)),
        ],
        compiler_params=pltpu.CompilerParams(vmem_limit_bytes=32 * 2**20),
        name="place_results",
    )(fresh, returned)
    return jnp.transpose(momentum_new, (1, 0, 2)), jnp.transpose(update, (1, 0, 2))


def solution(mesh):
    placed = P(None, ("dp", "tensor"), None)
    return jax.shard_map(
        on_device,
        mesh=mesh,
        in_specs=(placed, placed, P()),
        out_specs=(placed, placed),
        check_vma=False,
    )
```

```python
import math

import jax
import jax.numpy as jnp
from jax import lax
from jax.experimental import pallas as pl
from jax.experimental.pallas import tpu as pltpu
from jax.sharding import PartitionSpec as P

ITERS = 2
MESH = pl.DeviceIdType.MESH

momentum_rate = 0.95
epsilon_norm = 1e-07
linear_term = 3.4445
cubic_term = -4.775
quintic_term = 2.0315

SIDE = 4
CHIPS = SIDE**3
LOCAL = 6
WIDTH = 2560
LANES = 128
TILES = WIDTH // LANES
ROWS = LOCAL * CHIPS * 2
HALF = LOCAL * CHIPS
LINES = LOCAL * TILES
BLOCK = (8, LINES // 8 * LANES)
PITCH = LINES + 1
GROUP = 16
GROUPS = CHIPS // GROUP
PIECE = 4
PIECES = CHIPS // PIECE
SHARES = tuple((group, group + 1) for group in range(GROUPS))
TILE = 256
STRIPS = ROWS // TILE


def position():
    return lax.axis_index("dp"), lax.axis_index("tensor")


def hops_of(offset):
    return sum(min(step, SIDE - step) for step in offset)


def spread_offsets():
    sets = []
    for offset in ((x, y, z) for x in range(SIDE) for y in range(SIDE) for z in range(SIDE)):
        turns = [offset[turn:] + offset[:turn] for turn in range(3)]
        alike = dict.fromkeys(tuple(sign * step % SIDE for step in turn) for sign in (1, -1) for turn in turns)
        if offset == min(alike):
            sets.append(list(alike))
    hops = [hops_of(alike[0]) for alike in sets]
    ranked, rest = [], {}
    for index in range(1, len(sets)):
        rest.setdefault(hops[index], []).append(index)
    while any(rest.values()):
        for some in rest.values():
            if some:
                ranked.append(some.pop())
    return [offset for index in [0, *ranked] for offset in sets[index]]


OFFSETS = spread_offsets()


def targets(sign):
    place, _ = position()
    steps = []
    for scale in (SIDE * SIDE, SIDE, 1):
        here = place // scale % SIDE
        steps.append([(here + sign * away + SIDE) % SIDE * scale for away in range(SIDE)])
    return [steps[0][x] + steps[1][y] + steps[2][z] for x, y, z in OFFSETS]


def line_of(row, tile):
    return tile * LOCAL + row


def write_lines(scratch, row, tile, values):
    scratch[pl.ds(line_of(row, tile), 8, stride=PITCH), :] = values


def read_lines(scratch, row, tile):
    return scratch[pl.ds(line_of(row, tile), 8, stride=PITCH), :]


def pack_eight(scratch, blocks, first):
    for item in range(8):
        for part in range(LINES // 8):
            values = scratch[pl.ds(item * PITCH + 8 * part, 8), :]
            blocks[first + item, :, part * LANES : (part + 1) * LANES] = values.astype(jnp.bfloat16)


def unpack_eight(scratch, blocks, first):
    for item in range(8):
        values = blocks[first + item].astype(jnp.float32)
        for part in range(LINES // 8):
            scratch[pl.ds(item * PITCH + 8 * part, 8), :] = values[:, part * LANES : (part + 1) * LANES]


def product(a, b, dims):
    return lax.dot_general(a, b, (dims, ((), ())), preferred_element_type=jnp.float32)


def strip(index):
    return slice(index * TILE, (index + 1) * TILE)


def gram_block(x_ref, i, j):
    return product(x_ref[strip(i), :], x_ref[strip(j), :], ((1,), (1,)))


def keep_block(gram, low, i, j, value):
    gram[strip(i), strip(j)] = value
    low[strip(i), strip(j)] = value.astype(jnp.bfloat16)
    if i != j:
        low[strip(j), strip(i)] = value.T.astype(jnp.bfloat16)


def lay_out(lines, blocks, group, write, sums=None):
    for eight in range(2):
        unpack_eight(lines.at[eight], blocks, group * GROUP + eight * 8)
    for row in range(LOCAL):
        for tile in range(TILES):
            values = [read_lines(lines.at[eight], row, tile) for eight in range(2)]
            write(row, tile, jnp.concatenate(values, axis=0).astype(jnp.bfloat16))
            for index, value in enumerate(values if sums else ()):
                sums[2 * (tile % 2) + index] += value * value


def share_rows(group, core=0):
    return (2 * group + core) * LOCAL * GROUP


def mixer_of(gram, low, mixer, j):
    column = slice(j * TILE, ROWS)
    square = product(low[column, :], low[:, strip(j)], ((1,), (0,)))
    value = cubic_term * gram[column, strip(j)] + quintic_term * square
    mixer[column, strip(j)] = value.astype(jnp.bfloat16)
    for i in range(j + 1, STRIPS):
        mixer[strip(j), strip(i)] = value[strip(i - j), :].T.astype(jnp.bfloat16)


def kernel(
    momentum, gradient, assignment, momentum_new, returned,
    mom_in, grad_in, sent, arrived, relayed, x_now, x_next, gram, low, mixer, lines, squares, owners,
    plane_sem, owner_sem, load_sems, out_sem, in_sems, back_out_sem, back_sem, pair_out_sem, pair_sems,
):
    place, core = position()
    pair = (place, 1 - core)

    def load(group):
        rows = pl.ds(pl.multiple_of(group * GROUP, GROUP), GROUP)
        return (
            pltpu.make_async_copy(momentum.at[:, rows, :], mom_in.at[group], load_sems.at[0, group]),
            pltpu.make_async_copy(gradient.at[:, rows, :], grad_in.at[group], load_sems.at[1, group]),
        )

    for group in range(GROUPS):
        for copy in load(group):
            copy.start()
    fetch = pltpu.make_async_copy(assignment, owners, owner_sem)
    fetch.start()

    barrier = pltpu.get_barrier_semaphore()
    pl.semaphore_signal(barrier, inc=1, device_id=pair, device_id_type=MESH)

    ahead = targets(1)
    plane = [target for target, offset in zip(ahead, OFFSETS) if offset[2] == 0][1:]
    line = [target for target, offset in zip(ahead, OFFSETS) if offset[:2] == (0, 0)][1:]
    for target in plane + line:
        pl.semaphore_signal(barrier, inc=1, device_id=(target, core), device_id_type=MESH)

    def prepare(group, carry):
        for copy in load(group):
            copy.wait()
        rows = pl.ds(pl.multiple_of(group * GROUP, GROUP), GROUP)
        for row in range(LOCAL):
            for tile in range(TILES):
                columns = slice(tile * LANES, (tile + 1) * LANES)
                wide = grad_in[group, row, :, columns].astype(jnp.float32)
                fresh = momentum_rate * mom_in[group, row, :, columns] + wide
                momentum_new[row, rows, columns] = fresh
                direction = wide + momentum_rate * fresh
                for eight in range(2):
                    write_lines(lines.at[eight], row, tile, direction[eight * 8 : eight * 8 + 8])
        for eight in range(2):
            pack_eight(lines.at[eight], sent, group * GROUP + eight * 8)
        return carry

    lax.fori_loop(0, GROUPS // 2, prepare, 0)
    pl.semaphore_wait(barrier, 1 + len(plane) + len(line))
    for target in line:
        pl.semaphore_signal(plane_sem, inc=1, device_id=(target, core), device_id_type=MESH)
    lax.fori_loop(GROUPS // 2, GROUPS, prepare, 0)
    pl.semaphore_wait(plane_sem, len(line))

    pltpu.make_async_copy(sent.at[place], arrived.at[0], in_sems.at[0]).start()

    for slot, target in enumerate(ahead):
        if slot:
            pltpu.make_async_remote_copy(
                src_ref=sent.at[target], dst_ref=arrived.at[slot], send_sem=out_sem, recv_sem=in_sems.at[slot // PIECE],
                device_id=(target, core), device_id_type=MESH,
            ).start()

    def accept(blocks, group, which):
        def write(row, tile, values):
            start = share_rows(group, which) + row * GROUP
            x_now[start : start + GROUP, tile * LANES : (tile + 1) * LANES] = values

        sums = [jnp.zeros((8, LANES), jnp.float32)] * 4
        lay_out(lines, blocks, group, write, sums)
        squares[...] += (sums[0] + sums[1]) + (sums[2] + sums[3])

    def accept_pair(group):
        span = relayed.at[pl.ds(group * GROUP, GROUP)]
        pltpu.make_async_copy(span, span, pair_sems.at[group]).wait()
        accept(relayed, group, 1)
        for i in range(STRIPS - 1):
            if share_rows(group) < (i + 1) * TILE <= share_rows(group + 1):
                for j in range(i + 1):
                    gram[strip(i), strip(j)] = gram_block(x_now, i, j)

    squares[...] = jnp.zeros_like(squares)
    for group in range(GROUPS):
        if group:
            accept_pair(group - 1)
        for piece in range(group * GROUP // PIECE, (group + 1) * GROUP // PIECE):
            span = pl.ds(piece * PIECE, PIECE)
            pltpu.make_async_copy(arrived.at[span], arrived.at[span], in_sems.at[piece]).wait()
            pltpu.make_async_remote_copy(
                src_ref=arrived.at[span], dst_ref=relayed.at[span], send_sem=pair_out_sem, recv_sem=pair_sems.at[group],
                device_id=pair, device_id_type=MESH,
            ).start()
        accept(arrived, group, 0)
    accept_pair(GROUPS - 1)

    scale = 1.0 / (jnp.sqrt(jnp.sum(squares[...])) + epsilon_norm)

    def scaled(value):
        return jnp.where(scale > 0.0, value * scale * scale, 0.0)

    before = [(i, j) for i in range(STRIPS - 1) for j in range(i + 1)]
    for j in range(STRIPS):
        keep_block(gram, low, STRIPS - 1, j, scaled(gram_block(x_now, STRIPS - 1, j)))
        for i, k in before[j::STRIPS]:
            keep_block(gram, low, i, k, scaled(gram[strip(i), strip(k)]))

    for j in range(STRIPS):
        mixer_of(gram, low, mixer, j)

    for index in range(WIDTH // TILE):
        start = (x_now[:, strip(index)].astype(jnp.float32) * scale).astype(jnp.bfloat16)
        value = product(mixer[...], start, ((1,), (0,)))
        x_next[:, strip(index)] = (linear_term * start.astype(jnp.float32) + value).astype(jnp.bfloat16)

    for i in range(STRIPS):
        for j in range(i + 1):
            keep_block(gram, low, i, j, gram_block(x_next, i, j))

    fetch.wait()
    active = owners[place] >= 0
    made = set()

    def finish(first, last):
        for group in range(first, last):
            for j in range(STRIPS):
                if j not in made and share_rows(group) < (j + 1) * TILE and j * TILE < share_rows(group, 1):
                    made.add(j)
                    mixer_of(gram, low, mixer, j)
        rows = [slice(share_rows(group), share_rows(group, 1)) for group in range(first, last)]

        def gathered(ref):
            parts = [ref[row, :] for row in rows]
            return parts[0] if len(parts) == 1 else jnp.concatenate(parts, axis=0)

        value = linear_term * gathered(x_next).astype(jnp.float32) + product(
            gathered(mixer), x_next[...], ((1,), (0,))
        )
        value = math.sqrt(WIDTH) * value.astype(jnp.bfloat16).astype(jnp.float32)
        value = jnp.where(active, value, 0.0)
        for group in range(first, last):
            for eight in range(2):
                place_lines = lines.at[2 * (group - first) + eight]
                for row in range(LOCAL):
                    start = (group - first) * LOCAL * GROUP + row * GROUP + eight * 8
                    for tile in range(TILES):
                        write_lines(
                            place_lines, row, tile, value[start : start + 8, tile * LANES : (tile + 1) * LANES]
                        )
                pack_eight(place_lines, sent, group * GROUP + eight * 8)

    gone = sent.at[pl.ds(1, CHIPS - 1)]
    pltpu.make_async_copy(gone, gone, out_sem).wait()
    behind = targets(-1)
    for first, last in SHARES:
        finish(first, last)
        for slot in sorted(range(first * GROUP, last * GROUP), key=lambda slot: -hops_of(OFFSETS[slot])):
            if slot == 0:
                pltpu.make_async_copy(sent.at[0], returned.at[place], back_sem).start()
            else:
                pltpu.make_async_remote_copy(
                    src_ref=sent.at[slot], dst_ref=returned.at[place], send_sem=back_out_sem, recv_sem=back_sem,
                    device_id=(behind[slot], core), device_id_type=MESH,
                ).start()

    pltpu.make_async_copy(arrived, arrived, pair_out_sem).wait()
    pltpu.make_async_copy(returned, returned, back_sem).wait()
    pltpu.make_async_copy(gone, gone, back_out_sem).wait()


def place_results(fresh, returned, momentum_new, update, rows_out, lines, fresh_sem, group_sems):
    copies = [
        pltpu.make_async_copy(fresh.at[row], momentum_new.at[row], fresh_sem.at[row]) for row in range(LOCAL)
    ]
    for copy in copies:
        copy.start()
    for group in range(GROUPS):
        rows = pl.ds(group * GROUP, GROUP)

        def write(row, tile, values):
            rows_out[row, group * GROUP : (group + 1) * GROUP, tile * LANES : (tile + 1) * LANES] = values

        lay_out(lines, returned, group, write)
        copies.append(
            pltpu.make_async_copy(rows_out.at[:, rows, :], update.at[:, rows, :], group_sems.at[group])
        )
        copies[-1].start()
    for copy in copies:
        copy.wait()


def on_device(momentum, gradient, assignment):
    shape = (LOCAL, CHIPS, WIDTH)
    blocks = pltpu.VMEM((CHIPS, *BLOCK), jnp.bfloat16)
    line_space = pltpu.VMEM((2 * GROUPS, 9 * PITCH, LANES), jnp.float32)
    fresh, returned = pl.pallas_call(
        kernel,
        out_shape=(pltpu.VMEM(shape, jnp.float32), blocks),
        in_specs=[
            pl.BlockSpec(memory_space=pl.ANY),
            pl.BlockSpec(memory_space=pl.ANY),
            pl.BlockSpec(memory_space=pl.ANY),
        ],
        out_specs=[pl.BlockSpec(memory_space=pltpu.VMEM)] * 2,
        scratch_shapes=[
            pltpu.VMEM((GROUPS, LOCAL, GROUP, WIDTH), jnp.float32),
            pltpu.VMEM((GROUPS, LOCAL, GROUP, WIDTH), jnp.bfloat16),
            blocks,
            blocks,
            blocks,
            pltpu.VMEM((ROWS, WIDTH), jnp.bfloat16),
            pltpu.VMEM((ROWS, WIDTH), jnp.bfloat16),
            pltpu.VMEM((ROWS, ROWS), jnp.float32),
            pltpu.VMEM((ROWS, ROWS), jnp.bfloat16),
            pltpu.VMEM((ROWS, ROWS), jnp.bfloat16),
            line_space,
            pltpu.VMEM((8, LANES), jnp.float32),
            pltpu.SMEM((CHIPS,), jnp.int32),
            pltpu.SemaphoreType.REGULAR,
            pltpu.SemaphoreType.DMA,
            pltpu.SemaphoreType.DMA((2, GROUPS)),
            pltpu.SemaphoreType.DMA,
            pltpu.SemaphoreType.DMA((PIECES,)),
            pltpu.SemaphoreType.DMA,
            pltpu.SemaphoreType.DMA,
            pltpu.SemaphoreType.DMA,
            pltpu.SemaphoreType.DMA((GROUPS,)),
        ],
        compiler_params=pltpu.CompilerParams(
            collective_id=0, has_side_effects=True, vmem_limit_bytes=50 * 2**20
        ),
        name="muon",
    )(jnp.transpose(momentum, (1, 0, 2)), jnp.transpose(gradient, (1, 0, 2)), assignment)
    momentum_new, update = pl.pallas_call(
        place_results,
        out_shape=(jax.ShapeDtypeStruct(shape, jnp.float32), jax.ShapeDtypeStruct(shape, jnp.bfloat16)),
        in_specs=[pl.BlockSpec(memory_space=pltpu.VMEM)] * 2,
        out_specs=[pl.BlockSpec(memory_space=pl.ANY)] * 2,
        scratch_shapes=[
            pltpu.VMEM(shape, jnp.bfloat16),
            line_space,
            pltpu.SemaphoreType.DMA((LOCAL,)),
            pltpu.SemaphoreType.DMA((GROUPS,)),
        ],
        compiler_params=pltpu.CompilerParams(vmem_limit_bytes=32 * 2**20),
        name="place_results",
    )(fresh, returned)
    return jnp.transpose(momentum_new, (1, 0, 2)), jnp.transpose(update, (1, 0, 2))


def solution(mesh):
    placed = P(None, ("dp", "tensor"), None)
    return jax.shard_map(
        on_device,
        mesh=mesh,
        in_specs=(placed, placed, P()),
        out_specs=(placed, placed),
        check_vma=False,
    )
```
